512 devices in a mesh: grp: 16 (over z), pb: 32 (over x, y, core).
Axes of the slice: x: 4, y: 4, z: 16, core: 2. Of those that a mesh axis runs over, the one named last changes fastest.
Arguments:
- queries: bfloat16 [8192, 4096], P('grp', 'pb'), may hold values from -12 to 12
- outputs: bfloat16 [8192, 4096], P('grp', 'pb'), may hold values from -3 to 3
- readout_grad: bfloat16 [8192, 8192], P('grp', 'pb'), may hold values from -24 to 24
- readout_weight: bfloat16 [4096, 8192], P('pb'), may hold values from -0.125 to 0.125
- log_norm: float32 [8192, 32], P('grp', 'pb'), may hold values from 9 to 11
- probes: int32 [32, 8192, 4], P('pb', 'grp'), may hold values from 0 to 127, all different within a row; in each aligned block of 512 rows (0 to 511, 512 to 1023, ..., all dimensions but the last counted through in order) at most 32 rows name the same one
- owner_slots: int32 [32, 128], P('pb'), may hold values from 0 to 127, each once within a row
- counts: int32 [32, 128], P('pb', 'grp'), may hold values from 1 to 512
- cluster_keys: bfloat16 [32, 128, 512, 128], P('pb', 'grp'), may hold values from -6 to 6
- values: bfloat16 [32, 128, 512, 128], P('pb', 'grp'), may hold values from -6 to 6
Outputs:
- query_grad: bfloat16 [8192, 4096], P('grp', 'pb')
The draws below stay inside these ranges and needn't reach their ends.
Inputs may be any that keep to these rules, and one draw needn't show every extreme that they name: `probes`: each token names 4 different clusters for each head. Within the 512 tokens of one index of grp and one head, no cluster is named by more than 32 tokens, a bound that some block reaches. `owner_slots`: for each head a permutation of the 128 clusters; slot s is stored on index s // 8 of grp.
All inputs are finite; a program needn't handle non-finite values.
Results may differ from the reference program's by a relative error of at most 0.029.
Values may be sent and summed in bfloat16 or wider, within the bound.
No kernel may reach another device: no remote copies, remote signals or barrier semaphores. Data moves between devices by JAX's collectives and lax.ppermute only.
A program may use at most 64 MiB of HBM per device.

```python
import math
import jax
import jax.numpy as jnp
import numpy as np
from jax import lax

D = 8192
H = 32
DH = 128
S = 512
PROBES = 4
TOK_GRP = 512
NCL = 128
MOST = 32
TOKENS = 8192
N_GRP = 16


def touch_ends(result, key, smallest, largest):
    extent = result.shape
    spot = [jax.random.randint(jax.random.fold_in(key, axis), (), 0, extent[axis]) for axis in range(len(extent))]
    result = result.at[tuple(spot)].set(smallest)
    longest = extent.index(max(extent))
    spot[longest] = (spot[longest] + 1) % extent[longest]
    return result.at[tuple(spot)].set(largest)


def with_spikes(result, key, source, target, blocks, factor):
    owner, partner = [(jnp.arange(result.shape[dim]) // (result.shape[dim] // blocks)).reshape([-1 if axis == dim else 1 for axis in range(result.ndim)]) for dim in (source, target)]
    chosen = jax.random.permutation(key, blocks)[partner]
    strong = (owner == chosen) | (owner == (partner + blocks // 2) % blocks)
    return jnp.where(strong, factor * result, result)


def shard_levels(own_key, extent, cuts, smallest, largest):
    def one(dim, shards_of):
        steps = jax.random.uniform(jax.random.fold_in(jax.random.fold_in(own_key, 6), dim), (shards_of,), jnp.float32, smallest / len(cuts), largest / len(cuts))
        return jnp.repeat(jnp.exp(steps), extent[dim] // shards_of).reshape((-1,) + (1,) * (len(extent) - dim - 1))

    level = one(*cuts[0])
    for cut in cuts[1:]:
        level = level * one(*cut)
    return level


def assign_block(own_key, own, number, rows, count, top, limit, lean):
    order = jax.random.permutation(own_key, count)
    crowded, ordinary = shares(count, rows * top, limit, lean, True), shares(count, rows * top, limit, lean, False)
    places = jnp.arange(count)

    def named(lengths, turn):
        used = int((lengths > 0).sum())
        fixed = max(1, used // 4)
        shifted = fixed + (places - fixed + turn * (used - fixed)) % max(1, count - fixed)
        return jnp.zeros((count,), jnp.int32).at[order[jnp.where(places < fixed, places, shifted)]].set(jnp.asarray(lengths, jnp.int32))

    lengths = jnp.where(number % 4 == 0, named(crowded, number // 4), named(ordinary, number - number // 4 - 1))
    mixed = jax.random.permutation(jax.random.fold_in(own, 3), count)
    giver, taker = mixed[0:count // 2 * 2:2], mixed[1:count // 2 * 2:2]
    slack = jnp.minimum(lengths[giver] - 1, limit - lengths[taker]) // 2
    slack = jnp.where((giver == order[0]) | (taker == order[0]) | (lengths[taker] == 0), 0, jnp.maximum(slack, 0))
    shifted = jax.random.randint(jax.random.fold_in(own, 4), (count // 2,), 0, 1 << 20) % (slack + 1)
    lengths = lengths.at[giver].add(-shifted).at[taker].add(shifted)
    members = jnp.searchsorted(jnp.cumsum(lengths), jnp.arange(rows * top), side="right").astype(jnp.int32)
    listing = members.reshape(top, rows).T
    listing = listing[jax.random.permutation(jax.random.fold_in(own, 1), rows)]
    turn = jax.random.randint(jax.random.fold_in(own, 2), (rows, 1), 0, top)
    return jnp.take_along_axis(listing, (jnp.arange(top)[None, :] + turn) % top, axis=1)


def shares(number_of, total, reach, slope, full):
    weights = [(1 << 20) // math.isqrt(grade ** slope) + 1 for grade in range(1, number_of + 1)]
    largest = reach if full else min(reach, max(-(-total // number_of), total * weights[0] // sum(weights)))
    least = 1 if total - largest >= number_of - 1 else 0
    given, spare = [largest] + [least] * (number_of - 1), total - largest - least * (number_of - 1)
    while spare > 0:
        movable = [i for i in range(1, number_of) if given[i] < largest] or [i for i in range(1, number_of) if given[i] < reach]
        pool, left = sum([weights[i] for i in movable]), spare
        for i in movable:
            addition = min(reach - given[i], max(1, left * weights[i] // pool), spare)
            given[i] = given[i] + addition
            spare = spare - addition
    return np.array(given)


def scatter_about(stream_key, shape, deviation, limit, cuts=(), kind=jnp.bfloat16):
    array = jax.random.normal(stream_key, shape, jnp.float32) * deviation
    if len(cuts) > 0:
        array = shard_levels(stream_key, shape, cuts, -0.22, 0.18) * array
    return jnp.clip(array, min=-limit, max=limit).astype(kind)


def heavy_noise(own_key, dims, width, most, cuts, heavy, kind=jnp.bfloat16):
    values = width * jax.random.normal(own_key, dims, jnp.float32)
    if cuts:
        values = values * shard_levels(own_key, dims, cuts, -0.22, 0.18)
    return jnp.clip(with_spikes(values, jax.random.fold_in(own_key, 3), *heavy), -most, most).astype(kind)


def setup_inputs(seed: int = 0) -> dict:
    seeds = jax.random.split(jax.random.key(seed), 11)
    queries = scatter_about(seeds[0], (TOKENS, H * DH), 2.0, 12.0, ((0, 16), (1, 32)))
    outputs = scatter_about(seeds[1], (TOKENS, H * DH), 0.5, 3.0, ((0, 16), (1, 32)))
    readout_grad = scatter_about(seeds[2], (TOKENS, D), 4.0, 24.0, ((0, 16), (1, 32)))
    readout_weight = heavy_noise(seeds[3], (H * DH, D), D ** -0.5, 0.125, ((0, 32),), (1, 0, 32, 2.75))
    log_norm = jnp.clip(9.0 + 2.0 * jax.random.uniform(seeds[4], (TOKENS, H), jnp.float32) ** shard_levels(seeds[4], (TOKENS, H), ((0, 16), (1, 32)), -0.2, 0.2), 9.0, 11.0)
    probes_keys = jax.random.split(jax.random.fold_in(seeds[5], 1), H * TOKENS // TOK_GRP)
    probes_turns = jax.random.permutation(jax.random.fold_in(seeds[5], 3), H * TOKENS // TOK_GRP)
    probes = jax.vmap(lambda own, number: assign_block(jax.random.fold_in(seeds[5], 2), own, number, TOK_GRP, NCL, PROBES, MOST, 2))(probes_keys, probes_turns).reshape((H, TOKENS, PROBES))
    owner_slots = jax.vmap(lambda own: jax.random.permutation(own, NCL))(jax.random.split(seeds[6], H)).reshape((H, NCL)).astype(jnp.int32)
    counts = touch_ends(jax.random.randint(seeds[7], (H, NCL), 1, S + 1), jax.random.fold_in(seeds[7], 1), 1, S).astype(jnp.int32)
    cluster_keys = scatter_about(seeds[8], (H, NCL, S, DH), 1.0, 6.0, ((0, 32), (1, 16)))
    values = scatter_about(seeds[9], (H, NCL, S, DH), 1.0, 6.0, ((0, 32), (1, 16)))
    return dict(queries=queries, outputs=outputs, readout_grad=readout_grad, readout_weight=readout_weight, log_norm=log_norm, probes=probes, owner_slots=owner_slots, counts=counts, cluster_keys=cluster_keys, values=values)


def head_places(probe_ids, slot_table):
    slot_ids = slot_table[probe_ids].astype(jnp.int32)
    blocked = slot_ids.reshape(N_GRP, TOK_GRP, PROBES)
    cluster_ids = jnp.arange(NCL, dtype=jnp.int32)
    marked = lax.optimization_barrier(jnp.sum((blocked[..., None] == cluster_ids).astype(jnp.int32), axis=2, dtype=jnp.int32))
    before = jnp.cumsum(marked, axis=1, dtype=jnp.int32) - marked
    ranking = jnp.take_along_axis(before, blocked, axis=2).astype(jnp.int32)
    group_ids = jnp.arange(N_GRP, dtype=jnp.int32)[:, None, None]
    places = blocked * (N_GRP * MOST) + group_ids * MOST + ranking
    return places.reshape(TOKENS * PROBES).astype(jnp.int32)

def block_grad(pieces):
    query_block, grad_block, norm_block, delta_block, key_block, value_block, valid = pieces
    score_scale = DH ** (-0.5)
    scores = jnp.dot(query_block, key_block.T, preferred_element_type=jnp.float32) * score_scale
    valid_keys = jnp.arange(S, dtype=jnp.int32)[None, :] < valid
    weights = jnp.where(valid_keys, jnp.exp(scores - norm_block[:, None]), jnp.zeros_like(scores))
    grad_prob = jnp.dot(grad_block, value_block.T, preferred_element_type=jnp.float32)
    grad_score = (weights * (grad_prob - delta_block[:, None])).astype(jnp.bfloat16)
    return (jnp.dot(grad_score, key_block, preferred_element_type=jnp.float32) * score_scale).astype(jnp.bfloat16)

def reference(queries, outputs, readout_grad, readout_weight, log_norm, probes, owner_slots, counts, cluster_keys, values):
    grad_out = jnp.dot(readout_grad, readout_weight.T, preferred_element_type=jnp.float32).astype(jnp.bfloat16)
    row_delta = lax.optimization_barrier(jnp.sum((grad_out.astype(jnp.float32) * outputs.astype(jnp.float32)).reshape(TOKENS, H, DH), axis=2))
    query_heads = queries.reshape(TOKENS, H, DH).transpose(1, 0, 2)
    grad_heads = grad_out.reshape(TOKENS, H, DH).transpose(1, 0, 2)
    arrivals = N_GRP * MOST
    slot_total = NCL * arrivals

    def one_head(pieces):
        query_head, grad_head, norm_head, delta_head, probe_head, table_head, count_head, key_head, value_head = pieces
        places = head_places(probe_head, table_head)

        def spread(rows):
            repeated = jnp.repeat(rows, PROBES, axis=0)
            blank_rows = jnp.zeros((slot_total,) + rows.shape[1:], rows.dtype)
            return blank_rows.at[places].set(repeated).reshape((NCL, arrivals) + rows.shape[1:])
        partials = lax.map(block_grad, (spread(query_head), spread(grad_head), spread(norm_head), spread(delta_head), key_head, value_head, count_head))
        picked = partials.reshape(slot_total, DH)[places].reshape(TOKENS, PROBES, DH)
        return lax.optimization_barrier(jnp.sum(picked.astype(jnp.float32), axis=1)).astype(jnp.bfloat16)
    grads = lax.map(one_head, (query_heads, grad_heads, log_norm.T, row_delta.T, probes, owner_slots, counts, cluster_keys, values))
    return grads.transpose(1, 0, 2).reshape(TOKENS, H * DH)
```

```python
import functools

import jax
import jax.numpy as jnp
from jax import lax
from jax.experimental import pallas as pl
from jax.experimental.pallas import tpu as pltpu
from jax.sharding import PartitionSpec as P

F32 = jnp.float32
BF16 = jnp.bfloat16
EXTRA = 8
NT = (((1,), (1,)), ((), ()))
TN = (((0,), (0,)), ((), ()))
VMEM_BYTES = 48 * 1024 * 1024


def params():
    return pltpu.CompilerParams(vmem_limit_bytes=VMEM_BYTES)


def split_rows(row):
    high = row.astype(BF16).astype(F32)
    rest = row - high
    middle = rest.astype(BF16).astype(F32)
    low = (rest - middle).astype(BF16).astype(F32)
    pad = jnp.zeros((EXTRA - 3,) + row.shape[1:], F32)
    return jnp.concatenate([high, middle, low, pad], axis=0)


def store_extra(out_ref, extra, tokens):
    for i in range(0, tokens // 128, 2):
        both = [extra[:, (i + k) * 128 : (i + k + 1) * 128] for k in range(2)]
        start = tokens + i * EXTRA
        out_ref[start : start + 2 * EXTRA, :] = jnp.concatenate(both, axis=0).astype(BF16)


def rank_kernel(probes_ref, table_ref, ranks_ref):
    clusters, tokens = ranks_ref.shape[1:]
    probe_count = probes_ref.shape[1]
    cluster = lax.broadcasted_iota(jnp.int32, (clusters, tokens), 0)
    named = jnp.zeros((clusters, tokens), F32)
    for j in range(probe_count):
        named += jnp.where(probes_ref[0, j : j + 1, :] == cluster, 1.0, 0.0)
    slot = lax.broadcasted_iota(jnp.int32, (clusters, clusters), 0)
    table = jnp.where(table_ref[...] == slot, 1.0, 0.0).astype(BF16)
    marked = jnp.dot(table, named.astype(BF16), preferred_element_type=F32)
    earlier = lax.broadcasted_iota(jnp.int32, (tokens, tokens), 0)
    later = lax.broadcasted_iota(jnp.int32, (tokens, tokens), 1)
    before = jnp.where(earlier < later, 1.0, 0.0).astype(BF16)
    ranking = jnp.dot(marked.astype(BF16), before, preferred_element_type=F32)
    ranks_ref[0] = jnp.where(marked > 0.5, ranking, -1.0)


def rank_slots(probes_t, table):
    blocks, probe_count, tokens = probes_t.shape
    clusters = table.shape[1]
    return pl.pallas_call(
        rank_kernel,
        grid=(blocks,),
        in_specs=[
            pl.BlockSpec((1, probe_count, tokens), lambda b: (b, 0, 0)),
            pl.BlockSpec((1, clusters), lambda b: (0, 0)),
        ],
        out_specs=pl.BlockSpec((1, clusters, tokens), lambda b: (b, 0, 0)),
        out_shape=jax.ShapeDtypeStruct((blocks, clusters, tokens), F32),
        compiler_params=params(),
    )(probes_t, table)


def query_kernel(query_ref, norm_ref, out_ref):
    tokens = query_ref.shape[0]
    out_ref[0:tokens, :] = query_ref[...]
    store_extra(out_ref, split_rows(norm_ref[...]), tokens)


def query_payload(queries, norm_row):
    tokens, width = queries.shape
    return pl.pallas_call(
        query_kernel,
        out_shape=jax.ShapeDtypeStruct((tokens + EXTRA * tokens // 128, width), BF16),
        compiler_params=params(),
    )(queries, norm_row)


def grad_kernel(readout_ref, weight_ref, outputs_ref, out_ref, total_ref):
    step = pl.program_id(0)
    tokens = outputs_ref.shape[0]
    pieces, _, piece = readout_ref.shape

    @pl.when(step == 0)
    def _():
        total_ref[...] = jnp.zeros_like(total_ref)

    total = total_ref[...]
    for i in range(pieces):
        total += lax.dot_general(
            readout_ref[i],
            weight_ref[:, i * piece : (i + 1) * piece],
            NT,
            preferred_element_type=F32,
        )
    total_ref[...] = total

    @pl.when(step == pl.num_programs(0) - 1)
    def _():
        grad = total.astype(BF16)
        out_ref[0:tokens, :] = grad
        product = grad.astype(F32) * outputs_ref[...].astype(F32)
        delta = jnp.sum(product.T, axis=0, keepdims=True)
        store_extra(out_ref, split_rows(delta), tokens)


def grad_payload(readout, weight, outputs):
    shards_of, tokens, piece = readout.shape
    width = weight.shape[0]
    per_step = 4
    return pl.pallas_call(
        grad_kernel,
        grid=(shards_of // per_step,),
        in_specs=[
            pl.BlockSpec((per_step, tokens, piece), lambda i: (i, 0, 0)),
            pl.BlockSpec((width, per_step * piece), lambda i: (0, i)),
            pl.BlockSpec((tokens, width), lambda i: (0, 0)),
        ],
        out_specs=pl.BlockSpec((tokens + EXTRA * tokens // 128, width), lambda i: (0, 0)),
        out_shape=jax.ShapeDtypeStruct((tokens + EXTRA * tokens // 128, width), BF16),
        scratch_shapes=[pltpu.VMEM((tokens, width), F32)],
        compiler_params=params(),
    )(readout, weight, outputs)


def choices(ranks, capacity):
    slots, tokens = ranks.shape
    place = lax.broadcasted_iota(jnp.int32, (capacity, tokens), 0).astype(F32)
    rows = [jnp.where(ranks[s : s + 1, :] == place, 1.0, 0.0) for s in range(slots)]
    return jnp.concatenate(rows, axis=0).astype(BF16)


def gather_kernel(capacity, owners_ref, ranks_ref, payload_ref, out_ref):
    del owners_ref
    tokens = ranks_ref.shape[2]
    chosen = choices(ranks_ref[0], capacity)
    picked = chosen.shape[0]
    out_ref[0, 0, 0:picked, :] = jnp.dot(
        chosen, payload_ref[0, 0:tokens, :], preferred_element_type=F32
    ).astype(BF16)
    parts = [
        payload_ref[0, tokens + i * 2 * EXTRA : tokens + (i + 1) * 2 * EXTRA, :].astype(F32)
        for i in range(tokens // 256)
    ]
    wide = [part[k * EXTRA : (k + 1) * EXTRA] for part in parts for k in range(2)]
    extra = jnp.concatenate(wide, axis=1).astype(BF16)
    moved = lax.dot_general(extra, chosen, NT, preferred_element_type=F32)
    both = [moved[:, i * 128 : (i + 1) * 128] for i in range(picked // 128)]
    out_ref[0, 0, picked:, :] = jnp.concatenate(both, axis=0).astype(BF16)


def gather_rows(owners, ranks, payload, local_clusters, capacity):
    blocks, _, tokens = ranks.shape
    rows, width = payload.shape[1:]
    picked = local_clusters * capacity
    out_rows = picked + EXTRA * picked // 128
    return pl.pallas_call(
        functools.partial(gather_kernel, capacity),
        grid_spec=pltpu.PrefetchScalarGridSpec(
            num_scalar_prefetch=1,
            grid=(blocks, owners.shape[0]),
            in_specs=[
                pl.BlockSpec((1, local_clusters, tokens), lambda b, i, own: (b, own[i], 0)),
                pl.BlockSpec((1, rows, width), lambda b, i, own: (b, 0, 0)),
            ],
            out_specs=pl.BlockSpec((1, 1, out_rows, width), lambda b, i, own: (i, b, 0, 0)),
        ),
        out_shape=jax.ShapeDtypeStruct((owners.shape[0], blocks, out_rows, width), BF16),
        compiler_params=params(),
    )(owners, ranks, payload)


def scatter_kernel(capacity, owners_ref, ranks_ref, partial_ref, out_ref, total_ref):
    del owners_ref
    step = pl.program_id(1)
    chosen = choices(ranks_ref[0], capacity)
    added = lax.dot_general(partial_ref[0, 0], chosen, TN, preferred_element_type=F32)

    @pl.when(step == 0)
    def _():
        total_ref[...] = added

    @pl.when(step > 0)
    def _():
        total_ref[...] += added

    @pl.when(step == pl.num_programs(1) - 1)
    def _():
        out_ref[0] = total_ref[...].T.astype(BF16)


def scatter_rows(owners, ranks, partials, capacity):
    blocks, _, tokens = ranks.shape
    _, _, rows, width = partials.shape
    local_clusters = rows // capacity
    return pl.pallas_call(
        functools.partial(scatter_kernel, capacity),
        grid_spec=pltpu.PrefetchScalarGridSpec(
            num_scalar_prefetch=1,
            grid=(blocks, owners.shape[0]),
            in_specs=[
                pl.BlockSpec((1, local_clusters, tokens), lambda b, i, own: (b, own[i], 0)),
                pl.BlockSpec((1, 1, rows, width), lambda b, i, own: (i, b, 0, 0)),
            ],
            out_specs=pl.BlockSpec((1, tokens, width), lambda b, i, own: (b, 0, 0)),
            scratch_shapes=[pltpu.VMEM((width, tokens), F32)],
        ),
        out_shape=jax.ShapeDtypeStruct((blocks, tokens, width), BF16),
        compiler_params=params(),
    )(owners, ranks, partials)


def unpack_extra(extra_ref, rows_ref, capacity):
    senders = extra_ref.shape[0]
    per_row = 128 // capacity
    lane = lax.broadcasted_iota(jnp.int32, (2 * EXTRA, 128), 1) // capacity
    for sub in range(per_row):
        for group in range(senders // per_row):
            total = jnp.zeros((2 * EXTRA, 128), F32)
            for k in range(per_row):
                packed = extra_ref[group * per_row + k].astype(F32)
                turn = (k - sub) * capacity % 128
                if turn:
                    packed = pltpu.roll(packed, turn, 1)
                total += jnp.where(lane == k, packed, 0.0)
            lanes = slice(group * 128, (group + 1) * 128)
            for half in range(2):
                rows = total[half * EXTRA : half * EXTRA + 3]
                cluster = half * per_row + sub
                rows_ref[cluster : cluster + 1, lanes] = rows[0:1] + rows[1:2] + rows[2:3]


def block_kernel(
    capacity,
    counts_ref,
    query_ref,
    query_extra_ref,
    grad_ref,
    grad_extra_ref,
    key_ref,
    value_ref,
    out_ref,
    norm_ref,
    delta_ref,
):
    cluster = pl.program_id(0)
    senders, _, width = query_ref.shape
    span = key_ref.shape[2]
    arrivals = senders * capacity
    score_scale = width ** (-0.5)

    @pl.when(cluster == 0)
    def _():
        unpack_extra(query_extra_ref, norm_ref, capacity)
        unpack_extra(grad_extra_ref, delta_ref, capacity)

    keys, vals = key_ref[0, 0], value_ref[0, 0]
    query = query_ref[...].reshape(arrivals, width)
    grad = grad_ref[...].reshape(arrivals, width)
    scores = lax.dot_general(keys, query, NT, preferred_element_type=F32) * score_scale
    place = lax.broadcasted_iota(jnp.int32, (span, arrivals), 0)
    weights = jnp.where(
        place < counts_ref[cluster], jnp.exp(scores - norm_ref[pl.ds(cluster, 1), :]), 0.0
    )
    grad_prob = lax.dot_general(vals, grad, NT, preferred_element_type=F32)
    grad_score = (weights * (grad_prob - delta_ref[pl.ds(cluster, 1), :])).astype(BF16)
    partial = lax.dot_general(keys, grad_score, TN, preferred_element_type=F32) * score_scale
    out_ref[...] = partial.T.astype(BF16).reshape(senders, capacity, width)


def block_grads(counts, query_rows, grad_rows, keys, values, capacity):
    senders, _, width = query_rows.shape
    local_clusters, span = keys.shape[1:3]
    picked = local_clusters * capacity
    rows = pl.BlockSpec((senders, capacity, width), lambda c, _: (0, c, 0))
    extra = pl.BlockSpec(
        (senders, 2 * EXTRA, width), lambda c, _: (0, picked // (2 * EXTRA), 0)
    )
    stored = pl.BlockSpec((1, 1, span, width), lambda c, _: (0, c, 0, 0))
    return pl.pallas_call(
        functools.partial(block_kernel, capacity),
        grid_spec=pltpu.PrefetchScalarGridSpec(
            num_scalar_prefetch=1,
            grid=(local_clusters,),
            in_specs=[rows, extra, rows, extra, stored, stored],
            out_specs=rows,
            scratch_shapes=[pltpu.VMEM((local_clusters, senders * capacity), F32)] * 2,
        ),
        out_shape=jax.ShapeDtypeStruct((senders, picked, width), BF16),
        compiler_params=params(),
    )(counts, query_rows, query_rows, grad_rows, grad_rows, keys, values)


def shards(
    queries,
    outputs,
    readout_grad,
    readout_weight,
    log_norm,
    probes,
    owner_slots,
    counts,
    cluster_keys,
    values,
):
    token_count = queries.shape[0]
    probe_count = probes.shape[2]
    local_clusters = cluster_keys.shape[1]
    clusters = owner_slots.shape[1]
    capacity = 2 * token_count * probe_count // clusters
    owners = jnp.arange(lax.axis_size("grp"), dtype=jnp.int32)

    readout = lax.all_gather(readout_grad, "pb")
    ranks = rank_slots(probes.transpose(0, 2, 1), owner_slots)

    def dispatch(payload):
        rows = gather_rows(owners, ranks, payload[None], local_clusters, capacity)[:, 0]
        return lax.all_to_all(rows, "grp", split_axis=0, concat_axis=0)

    query_rows = dispatch(query_payload(queries, log_norm.reshape(1, token_count)))
    grad_rows = dispatch(grad_payload(readout, readout_weight, outputs))
    partials = block_grads(
        counts.reshape(local_clusters), query_rows, grad_rows, cluster_keys, values, capacity
    )
    returned = lax.all_to_all(partials, "grp", split_axis=0, concat_axis=0)
    return scatter_rows(owners, ranks, returned[:, None], capacity)[0]


def solution(mesh):
    placed = (
        P("grp", "pb"),
        P("grp", "pb"),
        P("grp", "pb"),
        P("pb", None),
        P("grp", "pb"),
        P("pb", "grp", None),
        P("pb", None),
        P("pb", "grp"),
        P("pb", "grp", None, None),
        P("pb", "grp", None, None),
    )
    return jax.shard_map(
        shards, mesh=mesh, in_specs=placed, out_specs=P("grp", "pb"), check_vma=False
    )
```

```python
import functools

import jax
import jax.numpy as jnp
from jax import lax
from jax.experimental import pallas as pl
from jax.experimental.pallas import tpu as pltpu
from jax.sharding import PartitionSpec as P

F32 = jnp.float32
BF16 = jnp.bfloat16
EXTRA = 8
NT = (((1,), (1,)), ((), ()))
TN = (((0,), (0,)), ((), ()))
SIDE, CORES = 4, 2
TURNS = (1, 3, 2)
SHARED = 4
NEAR = ((1, 1), (-1, -1), (2, -2))
VMEM_BYTES = 48 * 1024 * 1024


def params():
    return pltpu.CompilerParams(vmem_limit_bytes=VMEM_BYTES)


def split_rows(row):
    high = row.astype(BF16).astype(F32)
    rest = row - high
    middle = rest.astype(BF16).astype(F32)
    low = (rest - middle).astype(BF16).astype(F32)
    pad = jnp.zeros((EXTRA - 3,) + row.shape[1:], F32)
    return jnp.concatenate([high, middle, low, pad], axis=0)


def store_extra(out_ref, extra, tokens):
    for i in range(0, tokens // 128, 2):
        both = [extra[:, (i + k) * 128 : (i + k + 1) * 128] for k in range(2)]
        start = tokens + i * EXTRA
        out_ref[start : start + 2 * EXTRA, :] = jnp.concatenate(both, axis=0).astype(BF16)


def probe_rows(packed, tokens):
    packed, pieces = packed.astype(F32), tokens // 128
    return [
        jnp.concatenate([packed[j + i : j + i + 1] for i in range(pieces)], axis=1)
        for j in range(0, packed.shape[0], pieces)
    ]


def earlier_tokens(tokens):
    earlier = lax.broadcasted_iota(jnp.int32, (tokens, tokens), 0)
    later = lax.broadcasted_iota(jnp.int32, (tokens, tokens), 1)
    return jnp.where(earlier < later, 1.0, 0.0).astype(BF16)


def rank_kernel(table_ref, held_ref, packed_ref, ranks_ref):
    blocks, clusters, tokens = ranks_ref.shape
    cluster = lax.broadcasted_iota(jnp.int32, (clusters, tokens), 0).astype(F32)
    slot = lax.broadcasted_iota(jnp.int32, (clusters, clusters), 0)
    table = jnp.where(table_ref[...] == slot, 1.0, 0.0).astype(BF16)
    before = earlier_tokens(tokens)
    for b in range(blocks):
        named = jnp.zeros((clusters, tokens), F32)
        for row in probe_rows(packed_ref[held_ref[b]], tokens):
            named += jnp.where(row == cluster, 1.0, 0.0)
        marked = jnp.dot(table, named.astype(BF16), preferred_element_type=F32)
        ranking = jnp.dot(marked.astype(BF16), before, preferred_element_type=F32)
        ranks_ref[b] = jnp.where(marked > 0.5, ranking, -1.0)


def rank_slots(held, packed, table, tokens):
    blocks, clusters = held.shape[0], table.shape[1]
    return pl.pallas_call(
        rank_kernel,
        in_specs=[
            pl.BlockSpec(memory_space=pltpu.VMEM),
            pl.BlockSpec(memory_space=pltpu.SMEM),
            pl.BlockSpec(memory_space=pltpu.VMEM),
        ],
        out_shape=jax.ShapeDtypeStruct((blocks, clusters, tokens), F32),
        compiler_params=params(),
    )(table, held, packed)


def query_kernel(query_ref, norm_ref, probes_ref, out_ref):
    tokens = query_ref.shape[0]
    pieces = tokens // 128
    out_ref[0:tokens, :] = query_ref[...]
    store_extra(out_ref, split_rows(norm_ref[...]), tokens)
    probes = probes_ref[...].astype(F32)
    rows = [
        probes[j : j + 1, i * 128 : (i + 1) * 128]
        for j in range(probes.shape[0])
        for i in range(pieces)
    ]
    out_ref[tokens + EXTRA * pieces :, :] = jnp.concatenate(rows, axis=0).astype(BF16)


def query_payload(queries, norm_row, probes_t):
    tokens, width = queries.shape
    rows = tokens + (EXTRA + probes_t.shape[0]) * tokens // 128
    return pl.pallas_call(
        query_kernel,
        out_shape=jax.ShapeDtypeStruct((rows, width), BF16),
        compiler_params=params(),
    )(queries, norm_row, probes_t)


def weight_kernel(core_ref, weight_ref, own_ref, other_ref):
    pieces, _, piece = own_ref.shape
    core = core_ref[0]
    for i in range(pieces):
        for ref, side in ((own_ref, core), (other_ref, 1 - core)):
            start = pl.multiple_of((2 * i + side) * piece, piece)
            ref[i] = weight_ref[:, pl.ds(start, piece)]


def split_weight(core, weight, piece):
    width, depth = weight.shape
    half = jax.ShapeDtypeStruct((depth // piece // 2, width, piece), BF16)
    return pl.pallas_call(
        weight_kernel,
        in_specs=[
            pl.BlockSpec(memory_space=pltpu.SMEM),
            pl.BlockSpec(memory_space=pltpu.VMEM),
        ],
        out_shape=[half, half],
        compiler_params=params(),
    )(core, weight)


def product_kernel(first, count, added, order_ref, own_ref, other_ref, *refs):
    pieces, sums, results = refs[:count], refs[count : count + added], refs[count + added :]
    rows = results[0].shape[0] // 2
    for half in range(2):
        span = slice(half * rows, (half + 1) * rows)
        total = None
        for k, ref in enumerate(pieces):
            for m in range(ref.shape[0]):
                shard = order_ref[(first + k) * ref.shape[0] + m]
                both = jnp.concatenate([own_ref[shard], other_ref[shard]], axis=0)
                term = lax.dot_general(ref[m, span, :], both, NT, preferred_element_type=F32)
                total = term if total is None else total + term
        width = total.shape[1] // 2
        for i, out_ref in enumerate(results):
            part = total[:, i * width : (i + 1) * width]
            out_ref[span, :] = part + sums[i][span, :] if added else part


def partial_product(first, order, own, other, pieces, sums):
    result = jax.ShapeDtypeStruct((pieces[0].shape[1], own.shape[1]), F32)
    return pl.pallas_call(
        functools.partial(product_kernel, first, len(pieces), len(sums)),
        in_specs=[pl.BlockSpec(memory_space=pltpu.SMEM)]
        + [pl.BlockSpec(memory_space=pltpu.VMEM)] * (2 + len(pieces) + len(sums)),
        out_shape=[result, result],
        compiler_params=params(),
    )(order, own, other, *pieces, *sums)


def grad_kernel(own_ref, other_ref, outputs_ref, out_ref):
    tokens = outputs_ref.shape[0]
    grad = (own_ref[...] + other_ref[...]).astype(BF16)
    out_ref[0:tokens, :] = grad
    product = grad.astype(F32) * outputs_ref[...].astype(F32)
    delta = jnp.sum(product.T, axis=0, keepdims=True)
    store_extra(out_ref, split_rows(delta), tokens)


def grad_payload(own, other, outputs):
    tokens, width = outputs.shape
    return pl.pallas_call(
        grad_kernel,
        out_shape=jax.ShapeDtypeStruct((tokens + EXTRA * tokens // 128, width), BF16),
        compiler_params=params(),
    )(own, other, outputs)


def choices(ranks, capacity):
    slots, tokens = ranks.shape
    place = lax.broadcasted_iota(jnp.int32, (capacity, tokens), 0).astype(F32)
    rows = [jnp.where(ranks[s : s + 1, :] == place, 1.0, 0.0) for s in range(slots)]
    return jnp.concatenate(rows, axis=0).astype(BF16)


def owner_ranks(ranks_ref, block, owner, local_clusters):
    start = pl.multiple_of(owner * local_clusters, local_clusters)
    return ranks_ref[block, pl.ds(start, local_clusters), :]


def pick_rows(payload_ref, chosen, tokens, out_ref):
    picked = chosen.shape[0]
    parts = [
        payload_ref[tokens + i * 2 * EXTRA : tokens + (i + 1) * 2 * EXTRA, :].astype(F32)
        for i in range(tokens // 256)
    ]
    wide = [part[k * EXTRA : (k + 1) * EXTRA] for part in parts for k in range(2)]
    extra = jnp.concatenate(wide, axis=1).astype(BF16)
    out_ref[0:picked, :] = jnp.dot(
        chosen, payload_ref[0:tokens, :], preferred_element_type=F32
    ).astype(BF16)
    moved = lax.dot_general(extra, chosen, NT, preferred_element_type=F32)
    both = [moved[:, k * 128 : (k + 1) * 128] for k in range(picked // 128)]
    out_ref[picked:, :] = jnp.concatenate(both, axis=0).astype(BF16)


def gather_kernel(capacity, local_clusters, owners_ref, ranks_ref, payload_ref, *refs):
    blocks, _, tokens = ranks_ref.shape
    for b in range(blocks):
        for i, out_ref in enumerate(refs):
            chosen = choices(
                owner_ranks(ranks_ref, b, owners_ref[i], local_clusters), capacity
            )
            pick_rows(payload_ref.at[b], chosen, tokens, out_ref.at[b])


def gather_rows(owners, ranks, payloads, local_clusters, capacity):
    blocks, width = ranks.shape[0], payloads.shape[-1]
    picked = local_clusters * capacity
    rows = jax.ShapeDtypeStruct((blocks, picked + EXTRA * picked // 128, width), BF16)
    return pl.pallas_call(
        functools.partial(gather_kernel, capacity, local_clusters),
        in_specs=[pl.BlockSpec(memory_space=pltpu.SMEM)]
        + [pl.BlockSpec(memory_space=pltpu.VMEM)] * 2,
        out_shape=[rows] * owners.shape[0],
        compiler_params=params(),
    )(owners, ranks, payloads)


def own_kernel(capacity, tokens, group_ref, sources_ref, table_ref, payload_ref, *refs):
    sides = sources_ref.shape[0]
    blocks, out_rows, _ = refs[0].shape
    local_clusters = out_rows * 128 // (128 + EXTRA) // capacity
    clusters = table_ref.shape[1]
    slot = lax.broadcasted_iota(jnp.int32, (local_clusters, clusters), 0)
    cluster = lax.broadcasted_iota(jnp.int32, (local_clusters, clusters), 1)
    mine = table_ref[...] == slot + group_ref[0] * local_clusters
    stored = jnp.sum(jnp.where(mine, cluster.astype(F32), 0.0), axis=1, keepdims=True)
    start = tokens + EXTRA * tokens // 128
    marks = []
    for i in range(sides):
        for b in range(blocks):
            packed = payload_ref[sources_ref[i, b], start:, :]
            named = jnp.zeros((local_clusters, tokens), F32)
            for row in probe_rows(packed, tokens):
                named += jnp.where(row == stored, 1.0, 0.0)
            marks.append(named)
    marks = jnp.concatenate(marks, axis=0)
    ranking = jnp.dot(marks.astype(BF16), earlier_tokens(tokens), preferred_element_type=F32)
    ranks = jnp.where(marks > 0.5, ranking, -1.0)
    for i in range(sides):
        for b in range(blocks):
            first = (i * blocks + b) * local_clusters
            chosen = choices(ranks[first : first + local_clusters], capacity)
            pick_rows(payload_ref.at[sources_ref[i, b]], chosen, tokens, refs[i].at[b])


def own_rows(group, sources, table, payloads, tokens, local_clusters, capacity):
    sides, blocks = sources.shape
    picked = local_clusters * capacity
    width = payloads.shape[-1]
    rows = jax.ShapeDtypeStruct((blocks, picked + EXTRA * picked // 128, width), BF16)
    return pl.pallas_call(
        functools.partial(own_kernel, capacity, tokens),
        in_specs=[pl.BlockSpec(memory_space=pltpu.SMEM)] * 2
        + [pl.BlockSpec(memory_space=pltpu.VMEM)] * 2,
        out_shape=[rows] * sides,
        compiler_params=params(),
    )(group, sources, table, payloads)


def scatter_kernel(capacity, owners_ref, ranks_ref, *refs):
    partial_refs, out_ref = refs[:-1], refs[-1]
    local_clusters = partial_refs[0].shape[1] // capacity
    for b in range(ranks_ref.shape[0]):
        total = None
        for i, partial_ref in enumerate(partial_refs):
            chosen = choices(
                owner_ranks(ranks_ref, b, owners_ref[i], local_clusters), capacity
            )
            term = lax.dot_general(partial_ref[b], chosen, TN, preferred_element_type=F32)
            total = term if total is None else total + term
        out_ref[b] = total.T.astype(out_ref.dtype)


def scatter_rows(owners, ranks, partials, capacity):
    blocks, _, tokens = ranks.shape
    width = partials[0].shape[2]
    return pl.pallas_call(
        functools.partial(scatter_kernel, capacity),
        in_specs=[pl.BlockSpec(memory_space=pltpu.SMEM)]
        + [pl.BlockSpec(memory_space=pltpu.VMEM)] * (1 + len(partials)),
        out_shape=jax.ShapeDtypeStruct((blocks, tokens, width), BF16),
        compiler_params=params(),
    )(owners, ranks, *partials)


def unpack_extra(extra_refs, rows_ref, capacity):
    per_ref = extra_refs[0].shape[0]
    senders = per_ref * len(extra_refs)
    per_row = 128 // capacity
    lane = lax.broadcasted_iota(jnp.int32, (2 * EXTRA, 128), 1) // capacity
    for sub in range(per_row):
        for group in range(senders // per_row):
            total = jnp.zeros((2 * EXTRA, 128), F32)
            for k in range(per_row):
                sender = group * per_row + k
                packed = extra_refs[sender // per_ref][sender % per_ref].astype(F32)
                turn = (k - sub) * capacity % 128
                if turn:
                    packed = pltpu.roll(packed, turn, 1)
                total += jnp.where(lane == k, packed, 0.0)
            lanes = slice(group * 128, (group + 1) * 128)
            for half in range(2):
                rows = total[half * EXTRA : half * EXTRA + 3]
                cluster = half * per_row + sub
                rows_ref[cluster : cluster + 1, lanes] = rows[0:1] + rows[1:2] + rows[2:3]


def block_kernel(capacity, sides, counts_ref, *refs):
    query_refs, query_extras = refs[:sides], refs[sides : 2 * sides]
    grad_refs, grad_extras = refs[2 * sides : 3 * sides], refs[3 * sides : 4 * sides]
    key_ref, value_ref = refs[4 * sides : 4 * sides + 2]
    out_refs = refs[4 * sides + 2 : 5 * sides + 2]
    norm_ref, delta_ref = refs[5 * sides + 2 :]
    cluster = pl.program_id(0)
    senders, _, width = query_refs[0].shape
    span = key_ref.shape[2]
    score_scale = width ** (-0.5)
    each = senders * capacity
    arrivals = sides * each

    @pl.when(cluster == 0)
    def _():
        unpack_extra(query_extras, norm_ref, capacity)
        unpack_extra(grad_extras, delta_ref, capacity)

    keys, vals = key_ref[0, 0], value_ref[0, 0]
    query = jnp.concatenate([ref[...].reshape(each, width) for ref in query_refs], axis=0)
    grad = jnp.concatenate([ref[...].reshape(each, width) for ref in grad_refs], axis=0)
    scores = lax.dot_general(keys, query, NT, preferred_element_type=F32) * score_scale
    place = lax.broadcasted_iota(jnp.int32, (span, arrivals), 0)
    weights = jnp.where(
        place < counts_ref[cluster], jnp.exp(scores - norm_ref[pl.ds(cluster, 1), :]), 0.0
    )
    grad_prob = lax.dot_general(vals, grad, NT, preferred_element_type=F32)
    grad_score = (weights * (grad_prob - delta_ref[pl.ds(cluster, 1), :])).astype(BF16)
    partial = lax.dot_general(keys, grad_score, TN, preferred_element_type=F32) * score_scale
    partial = partial.T.astype(BF16)
    for i, out_ref in enumerate(out_refs):
        out_ref[...] = partial[i * each : (i + 1) * each].reshape(senders, capacity, width)


def block_grads(counts, query_rows, grad_rows, keys, values, capacity):
    sides = len(query_rows)
    senders, _, width = query_rows[0].shape
    local_clusters, span = keys.shape[1:3]
    picked = local_clusters * capacity
    rows = pl.BlockSpec((senders, capacity, width), lambda c, _: (0, c, 0))
    extra = pl.BlockSpec(
        (senders, 2 * EXTRA, width), lambda c, _: (0, picked // (2 * EXTRA), 0)
    )
    stored = pl.BlockSpec((1, 1, span, width), lambda c, _: (0, c, 0, 0))
    arrivals = sides * senders * capacity
    return pl.pallas_call(
        functools.partial(block_kernel, capacity, sides),
        grid_spec=pltpu.PrefetchScalarGridSpec(
            num_scalar_prefetch=1,
            grid=(local_clusters,),
            in_specs=([rows] * sides + [extra] * sides) * 2 + [stored, stored],
            out_specs=[rows] * sides,
            scratch_shapes=[pltpu.VMEM((local_clusters, arrivals), F32)] * 2,
        ),
        out_shape=[jax.ShapeDtypeStruct((senders, picked, width), BF16)] * sides,
        compiler_params=params(),
    )(counts, *query_rows, *query_rows, *grad_rows, *grad_rows, keys, values)


def plane_shift(array, turn, phase):
    pairs = []
    for x in range(SIDE):
        for y in range(SIDE):
            for core in range(CORES):
                across, along = (turn, 0) if core == phase else (0, turn)
                target = (x + across) % SIDE * SIDE + (y + along) % SIDE
                pairs.append(((x * SIDE + y) * CORES + core, target * CORES + core))
    return lax.ppermute(array, "pb", pairs)


def swap_cores(array):
    return lax.ppermute(array, "pb", [(i, i ^ 1) for i in range(SIDE * SIDE * CORES)])


def group_shift(array, steps):
    groups, width = lax.axis_size("grp"), lax.axis_size("pb")
    pairs = [
        (g * width + p, (g + steps[p % CORES]) % groups * width + p)
        for g in range(groups)
        for p in range(width)
    ]
    return lax.ppermute(array, ("grp", "pb"), pairs)


def exchange_far(blocks):
    groups, count = lax.axis_size("grp"), blocks.shape[0]
    apart = groups // count
    sets = [[g + apart * i for i in range(count)] for g in range(apart)]
    return lax.all_to_all(blocks, "grp", 0, 0, axis_index_groups=sets)


def share(payload):
    return exchange_far(jnp.broadcast_to(payload[None], (SHARED,) + payload.shape))


def shards(
    queries,
    outputs,
    readout_grad,
    readout_weight,
    log_norm,
    probes,
    owner_slots,
    counts,
    cluster_keys,
    values,
):
    token_count = queries.shape[0]
    probe_count = probes.shape[2]
    local_clusters = cluster_keys.shape[1]
    clusters = owner_slots.shape[1]
    capacity = 2 * token_count * probe_count // clusters
    groups = lax.axis_size("grp")
    group, place = lax.axis_index("grp"), lax.axis_index("pb")
    core, column, line = place % CORES, place // (CORES * SIDE), place // CORES % SIDE
    near = jnp.stack([0 * core, 0 * core + 1, 0 * core - 1, 2 - 4 * core])
    apart = groups // SHARED
    members = apart * jnp.arange(SHARED, dtype=jnp.int32)
    owners = (group + near) % groups
    held = group % apart + members
    sources = (group - near[:, None]) % groups % apart + members[None, :]

    payload = query_payload(queries, log_norm.reshape(1, token_count), probes[0].T)
    query_all = lax.all_gather(payload, "grp")

    piece = readout_grad.shape[1]
    first = jnp.stack([readout_grad] + [plane_shift(readout_grad, d, 0) for d in TURNS])
    own, other = split_weight(core.reshape(1), readout_weight, piece)
    other = swap_cores(other)
    second = [plane_shift(first, d, 1) for d in TURNS]
    turns = jnp.asarray((0,) + TURNS, jnp.int32)
    xs, ys = (column - turns) % SIDE, (line - turns) % SIDE
    order = jnp.where(
        core == 0,
        xs[None, :] * SIDE + ys[:, None],
        xs[:, None] * SIDE + ys[None, :],
    ).reshape(-1)
    sums = partial_product(0, order, own, other, [first], [])
    sums = partial_product(1, order, own, other, second, sums)
    grads_held = share(grad_payload(sums[0], swap_cores(sums[1]), outputs))

    packed = query_all[:, token_count + EXTRA * token_count // 128 :]
    ranks = rank_slots(held, packed, owner_slots, token_count)
    query_rows = own_rows(
        group.reshape(1), sources, owner_slots, query_all, token_count, local_clusters, capacity
    )
    rows = gather_rows(owners, ranks, grads_held, local_clusters, capacity)
    grad_rows = [rows[0]] + [group_shift(r, n) for r, n in zip(rows[1:], NEAR)]
    partials = block_grads(
        counts.reshape(local_clusters), query_rows, grad_rows, cluster_keys, values, capacity
    )
    returned = [partials[0]] + [
        group_shift(p, [-n for n in steps]) for p, steps in zip(partials[1:], NEAR)
    ]
    summed = exchange_far(scatter_rows(owners, ranks, returned, capacity))
    return jnp.sum(summed.astype(F32), axis=0).astype(BF16)


def solution(mesh):
    placed = (
        P("grp", "pb"),
        P("grp", "pb"),
        P("grp", "pb"),
        P("pb", None),
        P("grp", "pb"),
        P("pb", "grp", None),
        P("pb", None),
        P("pb", "grp"),
        P("pb", "grp", None, None),
        P("pb", "grp", None, None),
    )
    return jax.shard_map(
        shards, mesh=mesh, in_specs=placed, out_specs=P("grp", "pb"), check_vma=False
    )
```

```python
import functools

import jax
import jax.numpy as jnp
from jax import lax
from jax.experimental import pallas as pl
from jax.experimental.pallas import tpu as pltpu
from jax.sharding import PartitionSpec as P

F32 = jnp.float32
BF16 = jnp.bfloat16
EXTRA = 8
NT = (((1,), (1,)), ((), ()))
TN = (((0,), (0,)), ((), ()))
SIDE, CORES = 4, 2
TURNS = (1, 3, 2)
SHARED = 4
NEAR = ((1, 1), (-1, -1), (2, -2))
VMEM_BYTES = 48 * 1024 * 1024


def params():
    return pltpu.CompilerParams(vmem_limit_bytes=VMEM_BYTES)


def split_rows(row):
    high = row.astype(BF16).astype(F32)
    rest = row - high
    middle = rest.astype(BF16).astype(F32)
    low = (rest - middle).astype(BF16).astype(F32)
    pad = jnp.zeros((EXTRA - 3,) + row.shape[1:], F32)
    return jnp.concatenate([high, middle, low, pad], axis=0)


def store_extra(out_ref, extra, tokens):
    for i in range(0, tokens // 128, 2):
        both = [extra[:, (i + k) * 128 : (i + k + 1) * 128] for k in range(2)]
        start = tokens + i * EXTRA
        out_ref[start : start + 2 * EXTRA, :] = jnp.concatenate(both, axis=0).astype(BF16)


def probe_rows(packed, tokens):
    packed, pieces = packed.astype(F32), tokens // 128
    return [
        jnp.concatenate([packed[j + i : j + i + 1] for i in range(pieces)], axis=1)
        for j in range(0, packed.shape[0], pieces)
    ]


def earlier_tokens(tokens):
    earlier = lax.broadcasted_iota(jnp.int32, (tokens, tokens), 0)
    later = lax.broadcasted_iota(jnp.int32, (tokens, tokens), 1)
    return jnp.where(earlier < later, 1.0, 0.0).astype(BF16)


def rank_kernel(table_ref, held_ref, payload_ref, ranks_ref, packed_ref, arrived):
    blocks, clusters, tokens = ranks_ref.shape
    start = tokens + EXTRA * tokens // 128
    copies = [
        pltpu.make_async_copy(
            payload_ref.at[held_ref[b], pl.ds(start, packed_ref.shape[1]), :],
            packed_ref.at[b],
            arrived.at[b],
        )
        for b in range(blocks)
    ]
    for copy in copies:
        copy.start()
    cluster = lax.broadcasted_iota(jnp.int32, (clusters, tokens), 0).astype(F32)
    slot = lax.broadcasted_iota(jnp.int32, (clusters, clusters), 0)
    table = jnp.where(table_ref[...] == slot, 1.0, 0.0).astype(BF16)
    before = earlier_tokens(tokens)
    for b in range(blocks):
        copies[b].wait()
        named = jnp.zeros((clusters, tokens), F32)
        for row in probe_rows(packed_ref[b], tokens):
            named += jnp.where(row == cluster, 1.0, 0.0)
        marked = jnp.dot(table, named.astype(BF16), preferred_element_type=F32)
        ranking = jnp.dot(marked.astype(BF16), before, preferred_element_type=F32)
        ranks_ref[b] = jnp.where(marked > 0.5, ranking, -1.0)


def rank_slots(held, payloads, table, tokens):
    blocks, clusters = held.shape[0], table.shape[1]
    packed = payloads.shape[1] - tokens - EXTRA * tokens // 128
    return pl.pallas_call(
        rank_kernel,
        in_specs=[
            pl.BlockSpec(memory_space=pltpu.VMEM),
            pl.BlockSpec(memory_space=pltpu.SMEM),
            pl.BlockSpec(memory_space=pl.ANY),
        ],
        out_shape=jax.ShapeDtypeStruct((blocks, clusters, tokens), F32),
        scratch_shapes=[
            pltpu.VMEM((blocks, packed, 128), BF16),
            pltpu.SemaphoreType.DMA((blocks,)),
        ],
        compiler_params=params(),
    )(table, held, payloads)


def query_kernel(query_ref, norm_ref, probes_ref, out_ref):
    tokens = query_ref.shape[0]
    pieces = tokens // 128
    out_ref[0:tokens, :] = query_ref[...]
    store_extra(out_ref, split_rows(norm_ref[...]), tokens)
    probes = probes_ref[...].astype(F32)
    rows = [
        probes[j : j + 1, i * 128 : (i + 1) * 128]
        for j in range(probes.shape[0])
        for i in range(pieces)
    ]
    out_ref[tokens + EXTRA * pieces :, :] = jnp.concatenate(rows, axis=0).astype(BF16)


def query_payload(queries, norm_row, probes_t):
    tokens, width = queries.shape
    rows = tokens + (EXTRA + probes_t.shape[0]) * tokens // 128
    return pl.pallas_call(
        query_kernel,
        out_shape=jax.ShapeDtypeStruct((rows, width), BF16),
        compiler_params=params(),
    )(queries, norm_row, probes_t)


def weight_kernel(core_ref, weight_ref, own_ref, other_ref):
    pieces, _, piece = own_ref.shape
    core = core_ref[0]
    for i in range(pieces):
        for ref, side in ((own_ref, core), (other_ref, 1 - core)):
            start = pl.multiple_of((2 * i + side) * piece, piece)
            ref[i] = weight_ref[:, pl.ds(start, piece)]


def split_weight(core, weight, piece):
    width, depth = weight.shape
    half = jax.ShapeDtypeStruct((depth // piece // 2, width, piece), BF16)
    return pl.pallas_call(
        weight_kernel,
        in_specs=[
            pl.BlockSpec(memory_space=pltpu.SMEM),
            pl.BlockSpec(memory_space=pltpu.VMEM),
        ],
        out_shape=[half, half],
        compiler_params=params(),
    )(core, weight)


def product_kernel(first, count, added, order_ref, own_ref, other_ref, *refs):
    pieces, sums, results = refs[:count], refs[count : count + added], refs[count + added :]
    rows = results[0].shape[0] // 2
    for half in range(2):
        span = slice(half * rows, (half + 1) * rows)
        total = None
        for k, ref in enumerate(pieces):
            for m in range(ref.shape[0]):
                shard = order_ref[(first + k) * ref.shape[0] + m]
                both = jnp.concatenate([own_ref[shard], other_ref[shard]], axis=0)
                term = lax.dot_general(ref[m, span, :], both, NT, preferred_element_type=F32)
                total = term if total is None else total + term
        width = total.shape[1] // 2
        for i, out_ref in enumerate(results):
            part = total[:, i * width : (i + 1) * width]
            out_ref[span, :] = part + sums[i][span, :] if added else part


def partial_product(first, order, own, other, pieces, sums):
    result = jax.ShapeDtypeStruct((pieces[0].shape[1], own.shape[1]), F32)
    return pl.pallas_call(
        functools.partial(product_kernel, first, len(pieces), len(sums)),
        in_specs=[pl.BlockSpec(memory_space=pltpu.SMEM)]
        + [pl.BlockSpec(memory_space=pltpu.VMEM)] * (2 + len(pieces) + len(sums)),
        out_shape=[result, result],
        compiler_params=params(),
    )(order, own, other, *pieces, *sums)


def grad_kernel(own_ref, other_ref, outputs_ref, out_ref):
    tokens = outputs_ref.shape[0]
    grad = (own_ref[...] + other_ref[...]).astype(BF16)
    out_ref[0:tokens, :] = grad
    product = grad.astype(F32) * outputs_ref[...].astype(F32)
    delta = jnp.sum(product.T, axis=0, keepdims=True)
    store_extra(out_ref, split_rows(delta), tokens)


def grad_payload(own, other, outputs):
    tokens, width = outputs.shape
    return pl.pallas_call(
        grad_kernel,
        out_shape=jax.ShapeDtypeStruct((tokens + EXTRA * tokens // 128, width), BF16),
        compiler_params=params(),
    )(own, other, outputs)


def choices(ranks, capacity):
    slots, tokens = ranks.shape
    place = lax.broadcasted_iota(jnp.int32, (capacity, tokens), 0).astype(F32)
    rows = [jnp.where(ranks[s : s + 1, :] == place, 1.0, 0.0) for s in range(slots)]
    return jnp.concatenate(rows, axis=0).astype(BF16)


def owner_ranks(ranks_ref, block, owner, local_clusters):
    start = pl.multiple_of(owner * local_clusters, local_clusters)
    return ranks_ref[block, pl.ds(start, local_clusters), :]


def pick_rows(payload_ref, chosen, tokens, out_ref):
    picked = chosen.shape[0]
    parts = [
        payload_ref[tokens + i * 2 * EXTRA : tokens + (i + 1) * 2 * EXTRA, :].astype(F32)
        for i in range(tokens // 256)
    ]
    wide = [part[k * EXTRA : (k + 1) * EXTRA] for part in parts for k in range(2)]
    extra = jnp.concatenate(wide, axis=1).astype(BF16)
    out_ref[0:picked, :] = jnp.dot(
        chosen, payload_ref[0:tokens, :], preferred_element_type=F32
    ).astype(BF16)
    moved = lax.dot_general(extra, chosen, NT, preferred_element_type=F32)
    both = [moved[:, k * 128 : (k + 1) * 128] for k in range(picked // 128)]
    out_ref[picked:, :] = jnp.concatenate(both, axis=0).astype(BF16)


def gather_kernel(capacity, local_clusters, owners_ref, ranks_ref, payload_ref, *refs):
    blocks, _, tokens = ranks_ref.shape
    for b in range(blocks):
        for i, out_ref in enumerate(refs):
            chosen = choices(
                owner_ranks(ranks_ref, b, owners_ref[i], local_clusters), capacity
            )
            pick_rows(payload_ref.at[b], chosen, tokens, out_ref.at[b])


def gather_rows(owners, ranks, payloads, local_clusters, capacity):
    blocks, width = ranks.shape[0], payloads.shape[-1]
    picked = local_clusters * capacity
    rows = jax.ShapeDtypeStruct((blocks, picked + EXTRA * picked // 128, width), BF16)
    return pl.pallas_call(
        functools.partial(gather_kernel, capacity, local_clusters),
        in_specs=[pl.BlockSpec(memory_space=pltpu.SMEM)]
        + [pl.BlockSpec(memory_space=pltpu.VMEM)] * 2,
        out_shape=[rows] * owners.shape[0],
        compiler_params=params(),
    )(owners, ranks, payloads)


def own_kernel(capacity, tokens, group_ref, sources_ref, table_ref, payload_ref, *refs):
    sides = sources_ref.shape[0]
    blocks, out_rows, _ = refs[0].shape
    local_clusters = out_rows * 128 // (128 + EXTRA) // capacity
    clusters = table_ref.shape[1]
    slot = lax.broadcasted_iota(jnp.int32, (local_clusters, clusters), 0)
    cluster = lax.broadcasted_iota(jnp.int32, (local_clusters, clusters), 1)
    mine = table_ref[...] == slot + group_ref[0] * local_clusters
    stored = jnp.sum(jnp.where(mine, cluster.astype(F32), 0.0), axis=1, keepdims=True)
    start = tokens + EXTRA * tokens // 128
    marks = []
    for i in range(sides):
        for b in range(blocks):
            packed = payload_ref[sources_ref[i, b], start:, :]
            named = jnp.zeros((local_clusters, tokens), F32)
            for row in probe_rows(packed, tokens):
                named += jnp.where(row == stored, 1.0, 0.0)
            marks.append(named)
    marks = jnp.concatenate(marks, axis=0)
    ranking = jnp.dot(marks.astype(BF16), earlier_tokens(tokens), preferred_element_type=F32)
    ranks = jnp.where(marks > 0.5, ranking, -1.0)
    for i in range(sides):
        for b in range(blocks):
            first = (i * blocks + b) * local_clusters
            chosen = choices(ranks[first : first + local_clusters], capacity)
            pick_rows(payload_ref.at[sources_ref[i, b]], chosen, tokens, refs[i].at[b])


def own_rows(group, sources, table, payloads, tokens, local_clusters, capacity):
    sides, blocks = sources.shape
    picked = local_clusters * capacity
    width = payloads.shape[-1]
    rows = jax.ShapeDtypeStruct((blocks, picked + EXTRA * picked // 128, width), BF16)
    return pl.pallas_call(
        functools.partial(own_kernel, capacity, tokens),
        in_specs=[pl.BlockSpec(memory_space=pltpu.SMEM)] * 2
        + [pl.BlockSpec(memory_space=pltpu.VMEM)] * 2,
        out_shape=[rows] * sides,
        compiler_params=params(),
    )(group, sources, table, payloads)


def scatter_kernel(capacity, owners_ref, ranks_ref, *refs):
    partial_refs, out_ref = refs[:-1], refs[-1]
    local_clusters = partial_refs[0].shape[1] // capacity
    for b in range(ranks_ref.shape[0]):
        total = None
        for i, partial_ref in enumerate(partial_refs):
            chosen = choices(
                owner_ranks(ranks_ref, b, owners_ref[i], local_clusters), capacity
            )
            term = lax.dot_general(partial_ref[b], chosen, TN, preferred_element_type=F32)
            total = term if total is None else total + term
        out_ref[b] = total.T.astype(out_ref.dtype)


def scatter_rows(owners, ranks, partials, capacity):
    blocks, _, tokens = ranks.shape
    width = partials[0].shape[2]
    return pl.pallas_call(
        functools.partial(scatter_kernel, capacity),
        in_specs=[pl.BlockSpec(memory_space=pltpu.SMEM)]
        + [pl.BlockSpec(memory_space=pltpu.VMEM)] * (1 + len(partials)),
        out_shape=jax.ShapeDtypeStruct((blocks, tokens, width), BF16),
        compiler_params=params(),
    )(owners, ranks, *partials)


def unpack_extra(extra_refs, rows_ref, capacity):
    per_ref = extra_refs[0].shape[0]
    senders = per_ref * len(extra_refs)
    per_row = 128 // capacity
    lane = lax.broadcasted_iota(jnp.int32, (2 * EXTRA, 128), 1) // capacity
    for sub in range(per_row):
        for group in range(senders // per_row):
            total = jnp.zeros((2 * EXTRA, 128), F32)
            for k in range(per_row):
                sender = group * per_row + k
                packed = extra_refs[sender // per_ref][sender % per_ref].astype(F32)
                turn = (k - sub) * capacity % 128
                if turn:
                    packed = pltpu.roll(packed, turn, 1)
                total += jnp.where(lane == k, packed, 0.0)
            lanes = slice(group * 128, (group + 1) * 128)
            for half in range(2):
                rows = total[half * EXTRA : half * EXTRA + 3]
                cluster = half * per_row + sub
                rows_ref[cluster : cluster + 1, lanes] = rows[0:1] + rows[1:2] + rows[2:3]


def block_kernel(capacity, sides, counts_ref, *refs):
    query_refs, grad_refs = refs[:sides], refs[sides : 2 * sides]
    key_ref, value_ref = refs[2 * sides : 2 * sides + 2]
    out_refs = refs[2 * sides + 2 : 3 * sides + 2]
    norm_ref, delta_ref = refs[3 * sides + 2 :]
    senders, _, width = query_refs[0].shape
    local_clusters, span = key_ref.shape[1:3]
    score_scale = width ** (-0.5)
    each = senders * capacity
    arrivals = sides * each
    behind = slice(local_clusters * capacity, local_clusters * capacity + 2 * EXTRA)
    unpack_extra([ref.at[:, behind, :] for ref in query_refs], norm_ref, capacity)
    unpack_extra([ref.at[:, behind, :] for ref in grad_refs], delta_ref, capacity)
    place = lax.broadcasted_iota(jnp.int32, (span, arrivals), 0)

    for c in range(local_clusters):
        mine = slice(c * capacity, (c + 1) * capacity)
        query, grad = (
            jnp.concatenate([ref[:, mine, :].reshape(each, width) for ref in side], axis=0)
            for side in (query_refs, grad_refs)
        )
        keys = key_ref[0, c]
        scores = lax.dot_general(keys, query, NT, preferred_element_type=F32) * score_scale
        weights = jnp.where(
            place < counts_ref[c], jnp.exp(scores - norm_ref[c : c + 1, :]), 0.0
        )
        grad_prob = lax.dot_general(value_ref[0, c], grad, NT, preferred_element_type=F32)
        grad_score = (weights * (grad_prob - delta_ref[c : c + 1, :])).astype(BF16)
        partial = lax.dot_general(keys, grad_score, TN, preferred_element_type=F32)
        partial = (partial * score_scale).T.astype(BF16)
        for i, out_ref in enumerate(out_refs):
            rows = partial[i * each : (i + 1) * each]
            out_ref[:, mine, :] = rows.reshape(senders, capacity, width)


def block_grads(counts, query_rows, grad_rows, keys, values, capacity):
    sides = len(query_rows)
    senders, _, width = query_rows[0].shape
    local_clusters = keys.shape[1]
    picked = local_clusters * capacity
    arrivals = sides * senders * capacity
    return pl.pallas_call(
        functools.partial(block_kernel, capacity, sides),
        in_specs=[pl.BlockSpec(memory_space=pltpu.SMEM)]
        + [pl.BlockSpec(memory_space=pltpu.VMEM)] * (2 * sides + 2),
        out_shape=[jax.ShapeDtypeStruct((senders, picked, width), BF16)] * sides,
        scratch_shapes=[pltpu.VMEM((local_clusters, arrivals), F32)] * 2,
        compiler_params=params(),
    )(counts, *query_rows, *grad_rows, keys, values)


def plane_shift(array, turn, phase):
    pairs = []
    for x in range(SIDE):
        for y in range(SIDE):
            for core in range(CORES):
                across, along = (turn, 0) if core == phase else (0, turn)
                target = (x + across) % SIDE * SIDE + (y + along) % SIDE
                pairs.append(((x * SIDE + y) * CORES + core, target * CORES + core))
    return lax.ppermute(array, "pb", pairs)


def swap_cores(array):
    return lax.ppermute(array, "pb", [(i, i ^ 1) for i in range(SIDE * SIDE * CORES)])


def group_shift(array, steps):
    groups, width = lax.axis_size("grp"), lax.axis_size("pb")
    pairs = [
        (g * width + p, (g + steps[p % CORES]) % groups * width + p)
        for g in range(groups)
        for p in range(width)
    ]
    return lax.ppermute(array, ("grp", "pb"), pairs)


def far_sets():
    apart = lax.axis_size("grp") // SHARED
    return [[g + apart * i for i in range(SHARED)] for g in range(apart)]


def shards(
    queries,
    outputs,
    readout_grad,
    readout_weight,
    log_norm,
    probes,
    owner_slots,
    counts,
    cluster_keys,
    values,
):
    token_count = queries.shape[0]
    probe_count = probes.shape[2]
    local_clusters = cluster_keys.shape[1]
    clusters = owner_slots.shape[1]
    capacity = 2 * token_count * probe_count // clusters
    groups = lax.axis_size("grp")
    group, place = lax.axis_index("grp"), lax.axis_index("pb")
    core, column, line = place % CORES, place // (CORES * SIDE), place // CORES % SIDE
    near = jnp.stack([0 * core, 0 * core + 1, 0 * core - 1, 2 - 4 * core])
    apart = groups // SHARED
    members = apart * jnp.arange(SHARED, dtype=jnp.int32)
    owners = (group + near) % groups
    held = group % apart + members
    sources = (group - near[:, None]) % groups % apart + members[None, :]

    payload = query_payload(queries, log_norm.reshape(1, token_count), probes[0].T)
    query_all = lax.all_gather(payload, "grp")

    piece = readout_grad.shape[1]
    first = jnp.stack([readout_grad] + [plane_shift(readout_grad, d, 0) for d in TURNS])
    own, other = split_weight(core.reshape(1), readout_weight, piece)
    other = swap_cores(other)
    second = [plane_shift(first, d, 1) for d in TURNS]
    turns = jnp.asarray((0,) + TURNS, jnp.int32)
    xs, ys = (column - turns) % SIDE, (line - turns) % SIDE
    order = jnp.where(
        core == 0,
        xs[None, :] * SIDE + ys[:, None],
        xs[:, None] * SIDE + ys[None, :],
    ).reshape(-1)
    sums = []
    for i, pieces in enumerate([first] + second):
        sums = partial_product(i, order, own, other, [pieces], sums)
    payload = grad_payload(sums[0], swap_cores(sums[1]), outputs)
    grads_held = lax.all_gather(payload, "grp", axis_index_groups=far_sets())

    ranks = rank_slots(held, query_all, owner_slots, token_count)
    query_rows = own_rows(
        group.reshape(1), sources, owner_slots, query_all, token_count, local_clusters, capacity
    )
    rows = gather_rows(owners, ranks, grads_held, local_clusters, capacity)
    grad_rows = [rows[0]] + [group_shift(r, n) for r, n in zip(rows[1:], NEAR)]
    partials = block_grads(
        counts.reshape(local_clusters), query_rows, grad_rows, cluster_keys, values, capacity
    )
    returned = [partials[0]] + [
        group_shift(p, [-n for n in steps]) for p, steps in zip(partials[1:], NEAR)
    ]
    summed = scatter_rows(owners, ranks, returned, capacity)
    summed = lax.all_to_all(summed, "grp", 0, 0, axis_index_groups=far_sets())
    return jnp.sum(summed.astype(F32), axis=0).astype(BF16)


def solution(mesh):
    placed = (
        P("grp", "pb"),
        P("grp", "pb"),
        P("grp", "pb"),
        P("pb", None),
        P("grp", "pb"),
        P("pb", "grp", None),
        P("pb", None),
        P("pb", "grp"),
        P("pb", "grp", None, None),
        P("pb", "grp", None, None),
    )
    return jax.shard_map(
        shards, mesh=mesh, in_specs=placed, out_specs=P("grp", "pb"), check_vma=False
    )
```

```python
import functools

import jax
import jax.numpy as jnp
from jax import lax
from jax.experimental import pallas as pl
from jax.experimental.pallas import tpu as pltpu
from jax.sharding import PartitionSpec as P

F32 = jnp.float32
BF16 = jnp.bfloat16
EXTRA = 8
NT = (((1,), (1,)), ((), ()))
TN = (((0,), (0,)), ((), ()))
SIDE, CORES = 4, 2
TURNS = (1, 3, 2)
SHARED = 4
FIRST, SECOND = (1, 3), (3, 1)
NEAR = ((1, 1), (-1, -1), (2, -2))
VMEM_BYTES = 48 * 1024 * 1024


def params():
    return pltpu.CompilerParams(vmem_limit_bytes=VMEM_BYTES)


def split_rows(row):
    high = row.astype(BF16).astype(F32)
    rest = row - high
    middle = rest.astype(BF16).astype(F32)
    low = (rest - middle).astype(BF16).astype(F32)
    pad = jnp.zeros((EXTRA - 3,) + row.shape[1:], F32)
    return jnp.concatenate([high, middle, low, pad], axis=0)


def store_extra(out_ref, extra, tokens):
    for i in range(0, tokens // 128, 2):
        both = [extra[:, (i + k) * 128 : (i + k + 1) * 128] for k in range(2)]
        start = tokens + i * EXTRA
        out_ref[start : start + 2 * EXTRA, :] = jnp.concatenate(both, axis=0).astype(BF16)


def probe_rows(packed, tokens):
    packed, pieces = packed.astype(F32), tokens // 128
    return [
        jnp.concatenate([packed[j + i : j + i + 1] for i in range(pieces)], axis=1)
        for j in range(0, packed.shape[0], pieces)
    ]


def earlier_tokens(tokens):
    earlier = lax.broadcasted_iota(jnp.int32, (tokens, tokens), 0)
    later = lax.broadcasted_iota(jnp.int32, (tokens, tokens), 1)
    return jnp.where(earlier < later, 1.0, 0.0).astype(BF16)


def rank_kernel(table_ref, payload_ref, ranks_ref):
    blocks, clusters, tokens = ranks_ref.shape
    cluster = lax.broadcasted_iota(jnp.int32, (clusters, tokens), 0).astype(F32)
    slot = lax.broadcasted_iota(jnp.int32, (clusters, clusters), 0)
    table = jnp.where(table_ref[...] == slot, 1.0, 0.0).astype(BF16)
    before = earlier_tokens(tokens)
    start = tokens + EXTRA * tokens // 128
    for b in range(blocks):
        named = jnp.zeros((clusters, tokens), F32)
        for row in probe_rows(payload_ref[b, start:, :], tokens):
            named += jnp.where(row == cluster, 1.0, 0.0)
        marked = jnp.dot(table, named.astype(BF16), preferred_element_type=F32)
        ranking = jnp.dot(marked.astype(BF16), before, preferred_element_type=F32)
        ranks_ref[b] = jnp.where(marked > 0.5, ranking, -1.0)


def rank_slots(payloads, table, tokens):
    return pl.pallas_call(
        rank_kernel,
        out_shape=jax.ShapeDtypeStruct((payloads.shape[0], table.shape[1], tokens), F32),
        compiler_params=params(),
    )(table, payloads)


def query_kernel(query_ref, norm_ref, probes_ref, out_ref, packed_ref):
    tokens = query_ref.shape[0]
    pieces = tokens // 128
    out_ref[0:tokens, :] = query_ref[...]
    store_extra(out_ref, split_rows(norm_ref[...]), tokens)
    numbers = probes_ref[...].astype(F32)
    rows = [
        numbers[j : j + 1, i * 128 : (i + 1) * 128]
        for j in range(numbers.shape[0])
        for i in range(pieces)
    ]
    packed = jnp.concatenate(rows, axis=0).astype(BF16)
    out_ref[tokens + EXTRA * pieces :, :] = packed
    packed_ref[...] = packed


def query_payload(queries, norm_row, probes_t):
    tokens, width = queries.shape
    packed = probes_t.shape[0] * tokens // 128
    rows = tokens + EXTRA * tokens // 128 + packed
    return pl.pallas_call(
        query_kernel,
        out_shape=[
            jax.ShapeDtypeStruct((rows, width), BF16),
            jax.ShapeDtypeStruct((packed, 128), BF16),
        ],
        compiler_params=params(),
    )(queries, norm_row, probes_t)


def weight_kernel(core_ref, weight_ref, own_ref, other_ref):
    pieces, _, piece = own_ref.shape
    core = core_ref[0]
    for i in range(pieces):
        for ref, side in ((own_ref, core), (other_ref, 1 - core)):
            start = pl.multiple_of((2 * i + side) * piece, piece)
            ref[i] = weight_ref[:, pl.ds(start, piece)]


def split_weight(core, weight, piece):
    width, depth = weight.shape
    half = jax.ShapeDtypeStruct((depth // piece // 2, width, piece), BF16)
    return pl.pallas_call(
        weight_kernel,
        in_specs=[
            pl.BlockSpec(memory_space=pltpu.SMEM),
            pl.BlockSpec(memory_space=pltpu.VMEM),
        ],
        out_shape=[half, half],
        compiler_params=params(),
    )(core, weight)


def product_kernel(turn, order_ref, own_ref, other_ref, *refs):
    halves, sums, results = refs[:2], refs[2:-2], refs[-2:]
    rows = halves[0].shape[1]
    for half, ref in enumerate(halves):
        span = slice(half * rows, (half + 1) * rows)
        total = None
        for m in range(ref.shape[0]):
            shard = order_ref[turn * ref.shape[0] + m]
            both = jnp.concatenate([own_ref[shard], other_ref[shard]], axis=0)
            term = lax.dot_general(ref[m], both, NT, preferred_element_type=F32)
            total = term if total is None else total + term
        width = total.shape[1] // 2
        for i, out_ref in enumerate(results):
            part = total[:, i * width : (i + 1) * width]
            out_ref[span, :] = part + sums[i][span, :] if sums else part


def partial_product(turn, order, own, other, halves, sums):
    result = jax.ShapeDtypeStruct((2 * halves[0].shape[1], own.shape[1]), F32)
    return pl.pallas_call(
        functools.partial(product_kernel, turn),
        in_specs=[pl.BlockSpec(memory_space=pltpu.SMEM)]
        + [pl.BlockSpec(memory_space=pltpu.VMEM)] * (4 + len(sums)),
        out_shape=[result, result],
        compiler_params=params(),
    )(order, own, other, *halves, *sums)


def grad_kernel(own_ref, other_ref, outputs_ref, packed_ref, out_ref):
    tokens = outputs_ref.shape[0]
    grad = (own_ref[...] + other_ref[...]).astype(BF16)
    out_ref[0:tokens, :] = grad
    product = grad.astype(F32) * outputs_ref[...].astype(F32)
    delta = jnp.sum(product.T, axis=0, keepdims=True)
    store_extra(out_ref, split_rows(delta), tokens)
    out_ref[tokens + EXTRA * tokens // 128 :, :] = packed_ref[...]


def grad_payload(own, other, outputs, packed):
    tokens, width = outputs.shape
    rows = tokens + EXTRA * tokens // 128 + packed.shape[0]
    return pl.pallas_call(
        grad_kernel,
        out_shape=jax.ShapeDtypeStruct((rows, width), BF16),
        compiler_params=params(),
    )(own, other, outputs, packed)


def choices(ranks, capacity):
    slots, tokens = ranks.shape
    place = lax.broadcasted_iota(jnp.int32, (capacity, tokens), 0).astype(F32)
    rows = [jnp.where(ranks[s : s + 1, :] == place, 1.0, 0.0) for s in range(slots)]
    return jnp.concatenate(rows, axis=0).astype(BF16)


def owner_ranks(ranks_ref, block, owner, local_clusters):
    start = pl.multiple_of(owner * local_clusters, local_clusters)
    return ranks_ref[block, pl.ds(start, local_clusters), :]


def pick_rows(payload_ref, chosen, tokens, out_ref):
    picked = chosen.shape[0]
    parts = [
        payload_ref[tokens + i * 2 * EXTRA : tokens + (i + 1) * 2 * EXTRA, :].astype(F32)
        for i in range(tokens // 256)
    ]
    wide = [part[k * EXTRA : (k + 1) * EXTRA] for part in parts for k in range(2)]
    extra = jnp.concatenate(wide, axis=1).astype(BF16)
    out_ref[0:picked, :] = jnp.dot(
        chosen, payload_ref[0:tokens, :], preferred_element_type=F32
    ).astype(BF16)
    moved = lax.dot_general(extra, chosen, NT, preferred_element_type=F32)
    both = [moved[:, k * 128 : (k + 1) * 128] for k in range(picked // 128)]
    out_ref[picked:, :] = jnp.concatenate(both, axis=0).astype(BF16)


def gather_kernel(capacity, local_clusters, owners_ref, ranks_ref, payload_ref, *refs):
    blocks, _, tokens = ranks_ref.shape
    for b in range(blocks):
        for i, out_ref in enumerate(refs):
            chosen = choices(
                owner_ranks(ranks_ref, b, owners_ref[i], local_clusters), capacity
            )
            pick_rows(payload_ref.at[b], chosen, tokens, out_ref.at[b])


def gather_rows(owners, ranks, payloads, local_clusters, capacity):
    blocks, width = ranks.shape[0], payloads.shape[-1]
    picked = local_clusters * capacity
    rows = jax.ShapeDtypeStruct((blocks, picked + EXTRA * picked // 128, width), BF16)
    return pl.pallas_call(
        functools.partial(gather_kernel, capacity, local_clusters),
        in_specs=[pl.BlockSpec(memory_space=pltpu.SMEM)]
        + [pl.BlockSpec(memory_space=pltpu.VMEM)] * 2,
        out_shape=[rows] * owners.shape[0],
        compiler_params=params(),
    )(owners, ranks, payloads)


def own_kernel(capacity, tokens, group_ref, sources_ref, table_ref, payload_ref, *refs):
    places = [(i, b) for i, ref in enumerate(refs) for b in range(ref.shape[0])]
    local_clusters = refs[0].shape[1] * 128 // (128 + EXTRA) // capacity
    clusters = table_ref.shape[1]
    slot = lax.broadcasted_iota(jnp.int32, (local_clusters, clusters), 0)
    cluster = lax.broadcasted_iota(jnp.int32, (local_clusters, clusters), 1)
    mine = table_ref[...] == slot + group_ref[0] * local_clusters
    stored = jnp.sum(jnp.where(mine, cluster.astype(F32), 0.0), axis=1, keepdims=True)
    start = tokens + EXTRA * tokens // 128
    marks = []
    for k in range(len(places)):
        named = jnp.zeros((local_clusters, tokens), F32)
        for row in probe_rows(payload_ref[sources_ref[k], start:, :], tokens):
            named += jnp.where(row == stored, 1.0, 0.0)
        marks.append(named)
    marks = jnp.concatenate(marks, axis=0)
    ranking = jnp.dot(marks.astype(BF16), earlier_tokens(tokens), preferred_element_type=F32)
    ranks = jnp.where(marks > 0.5, ranking, -1.0)
    for k, (i, b) in enumerate(places):
        chosen = choices(ranks[k * local_clusters : (k + 1) * local_clusters], capacity)
        pick_rows(payload_ref.at[sources_ref[k]], chosen, tokens, refs[i].at[b])


def own_rows(group, sources, counts, table, payloads, tokens, local_clusters, capacity):
    picked = local_clusters * capacity
    width = payloads.shape[-1]
    rows = [(count, picked + EXTRA * picked // 128, width) for count in counts]
    return pl.pallas_call(
        functools.partial(own_kernel, capacity, tokens),
        in_specs=[pl.BlockSpec(memory_space=pltpu.SMEM)] * 2
        + [pl.BlockSpec(memory_space=pltpu.VMEM)] * 2,
        out_shape=[jax.ShapeDtypeStruct(shape, BF16) for shape in rows],
        compiler_params=params(),
    )(group, sources, table, payloads)


def scatter_kernel(capacity, owners_ref, held_ref, ranks_ref, *refs):
    partial_refs, (own_ref, pair_ref, kept_ref) = refs[:-3], refs[-3:]
    local_clusters = partial_refs[0].shape[1] // capacity
    places = (own_ref, pair_ref.at[0], kept_ref, pair_ref.at[1])
    for k in (1, 3, 2, 0):
        b = held_ref[k]
        total = None
        for i, partial_ref in enumerate(partial_refs):
            chosen = choices(
                owner_ranks(ranks_ref, b, owners_ref[i], local_clusters), capacity
            )
            term = lax.dot_general(partial_ref[b], chosen, TN, preferred_element_type=F32)
            total = term if total is None else total + term
        places[k][...] = total.T.astype(places[k].dtype)


def scatter_rows(owners, held, ranks, partials, capacity):
    tokens, width = ranks.shape[2], partials[0].shape[2]
    return pl.pallas_call(
        functools.partial(scatter_kernel, capacity),
        in_specs=[pl.BlockSpec(memory_space=pltpu.SMEM)] * 2
        + [pl.BlockSpec(memory_space=pltpu.VMEM)] * (1 + len(partials)),
        out_shape=[
            jax.ShapeDtypeStruct((tokens, width), F32),
            jax.ShapeDtypeStruct((2, tokens, width), BF16),
            jax.ShapeDtypeStruct((tokens, width), F32),
        ],
        compiler_params=params(),
    )(owners, held, ranks, *partials)


def unpack_extra(extra_refs, rows_ref, capacity):
    places = [(i, b) for i, ref in enumerate(extra_refs) for b in range(ref.shape[0])]
    senders = len(places)
    per_row = 128 // capacity
    lane = lax.broadcasted_iota(jnp.int32, (2 * EXTRA, 128), 1) // capacity
    for sub in range(per_row):
        for group in range(senders // per_row):
            total = jnp.zeros((2 * EXTRA, 128), F32)
            for k in range(per_row):
                side, sender = places[group * per_row + k]
                packed = extra_refs[side][sender].astype(F32)
                turn = (k - sub) * capacity % 128
                if turn:
                    packed = pltpu.roll(packed, turn, 1)
                total += jnp.where(lane == k, packed, 0.0)
            lanes = slice(group * 128, (group + 1) * 128)
            for half in range(2):
                rows = total[half * EXTRA : half * EXTRA + 3]
                cluster = half * per_row + sub
                rows_ref[cluster : cluster + 1, lanes] = rows[0:1] + rows[1:2] + rows[2:3]


def block_kernel(capacity, sides, counts_ref, *refs):
    query_refs, grad_refs = refs[:sides], refs[sides : 2 * sides]
    key_ref, value_ref = refs[2 * sides : 2 * sides + 2]
    out_refs = refs[2 * sides + 2 : 3 * sides + 2]
    norm_ref, delta_ref = refs[3 * sides + 2 :]
    width = query_refs[0].shape[2]
    local_clusters, span = key_ref.shape[1:3]
    score_scale = width ** (-0.5)
    arrivals = norm_ref.shape[1]
    behind = slice(local_clusters * capacity, local_clusters * capacity + 2 * EXTRA)
    unpack_extra([ref.at[:, behind, :] for ref in query_refs], norm_ref, capacity)
    unpack_extra([ref.at[:, behind, :] for ref in grad_refs], delta_ref, capacity)
    place = lax.broadcasted_iota(jnp.int32, (span, arrivals), 0)

    for c in range(local_clusters):
        mine = slice(c * capacity, (c + 1) * capacity)
        query, grad = (
            jnp.concatenate([ref[:, mine, :].reshape(-1, width) for ref in side], axis=0)
            for side in (query_refs, grad_refs)
        )
        keys = key_ref[0, c]
        scores = lax.dot_general(keys, query, NT, preferred_element_type=F32) * score_scale
        weights = jnp.where(
            place < counts_ref[c], jnp.exp(scores - norm_ref[c : c + 1, :]), 0.0
        )
        grad_prob = lax.dot_general(value_ref[0, c], grad, NT, preferred_element_type=F32)
        grad_score = (weights * (grad_prob - delta_ref[c : c + 1, :])).astype(BF16)
        partial = lax.dot_general(keys, grad_score, TN, preferred_element_type=F32)
        partial = (partial * score_scale).T.astype(BF16)
        start = 0
        for out_ref in out_refs:
            stop = start + out_ref.shape[0] * capacity
            out_ref[:, mine, :] = partial[start:stop].reshape(-1, capacity, width)
            start = stop


def block_grads(counts, query_rows, grad_rows, keys, values, capacity):
    sides = len(query_rows)
    width = query_rows[0].shape[2]
    local_clusters = keys.shape[1]
    picked = local_clusters * capacity
    senders = [rows.shape[0] for rows in query_rows]
    arrivals = sum(senders) * capacity
    return pl.pallas_call(
        functools.partial(block_kernel, capacity, sides),
        in_specs=[pl.BlockSpec(memory_space=pltpu.SMEM)]
        + [pl.BlockSpec(memory_space=pltpu.VMEM)] * (2 * sides + 2),
        out_shape=[jax.ShapeDtypeStruct((count, picked, width), BF16) for count in senders],
        scratch_shapes=[pltpu.VMEM((local_clusters, arrivals), F32)] * 2,
        compiler_params=params(),
    )(counts, *query_rows, *grad_rows, keys, values)


def plane_shift(array, turn, phase):
    pairs = []
    for x in range(SIDE):
        for y in range(SIDE):
            for core in range(CORES):
                across, along = (turn, 0) if core == phase else (0, turn)
                target = (x + across) % SIDE * SIDE + (y + along) % SIDE
                pairs.append(((x * SIDE + y) * CORES + core, target * CORES + core))
    return lax.ppermute(array, "pb", pairs)


def swap_cores(array):
    return lax.ppermute(array, "pb", [(i, i ^ 1) for i in range(SIDE * SIDE * CORES)])


def group_shift(array, *steps):
    groups, width = lax.axis_size("grp"), lax.axis_size("pb")
    pairs = [
        (g * width + p, (g + steps[p % len(steps)]) % groups * width + p)
        for g in range(groups)
        for p in range(width)
    ]
    return lax.ppermute(array, ("grp", "pb"), pairs)


def partner_swap(array, partner):
    groups, width = lax.axis_size("grp"), lax.axis_size("pb")
    apart = groups // SHARED
    pairs = [
        (g * width + p, (g ^ (partner[p % CORES] * apart)) * width + p)
        for g in range(groups)
        for p in range(width)
    ]
    return lax.ppermute(array, ("grp", "pb"), pairs)


def shards(
    queries,
    outputs,
    readout_grad,
    readout_weight,
    log_norm,
    probes,
    owner_slots,
    counts,
    cluster_keys,
    values,
):
    token_count = queries.shape[0]
    probe_count = probes.shape[2]
    local_clusters = cluster_keys.shape[1]
    clusters = owner_slots.shape[1]
    capacity = 2 * token_count * probe_count // clusters
    groups = lax.axis_size("grp")
    group, place = lax.axis_index("grp"), lax.axis_index("pb")
    core, column, line = place % CORES, place // (CORES * SIDE), place // CORES % SIDE
    apart = groups // SHARED
    sets = [[g + apart * i for i in range(SHARED)] for g in range(apart)]
    near = [0, 1, -1, 2 - 4 * core]
    owners = jnp.stack([(group + n) % groups for n in near])
    sources = [(group - n) % groups % apart + apart * b for n in near for b in range(SHARED)]

    payload, packed = query_payload(queries, log_norm.reshape(1, token_count), probes[0].T)
    query_all = lax.all_gather(payload, "grp")

    piece = readout_grad.shape[1]
    first = [readout_grad] + [plane_shift(readout_grad, d, 0) for d in TURNS]
    half = token_count // 2
    upper = jnp.stack([p[:half] for p in first])
    lower = jnp.stack([p[half:] for p in first])
    own, other = split_weight(core.reshape(1), readout_weight, piece)
    other = swap_cores(other)
    before_up, after_low = plane_shift(upper, 1, 1), plane_shift(lower, -1, 1)
    before_low, after_up = plane_shift(lower, 1, 1), plane_shift(upper, -1, 1)
    far_up, far_low = plane_shift(before_up, 1, 1), plane_shift(after_low, -1, 1)
    turns = jnp.asarray((0,) + TURNS, jnp.int32)
    xs, ys = (column - turns) % SIDE, (line - turns) % SIDE
    order = jnp.where(
        core == 0,
        xs[None, :] * SIDE + ys[:, None],
        xs[:, None] * SIDE + ys[None, :],
    ).reshape(-1)
    arrivals = [(upper, lower), (before_up, before_low), (after_up, after_low), (far_up, far_low)]
    sums = []
    for turn, halves in enumerate(arrivals):
        sums = partial_product(turn, order, own, other, halves, sums)
    payload = grad_payload(sums[0], swap_cores(sums[1]), outputs, packed)
    held = lax.all_gather(payload, "grp", axis_index_groups=sets)
    ranks = rank_slots(held, owner_slots, token_count)
    grad_rows = []
    for i, n in enumerate(NEAR):
        (rows,) = gather_rows(owners[i + 1 : i + 2], ranks, held, local_clusters, capacity)
        grad_rows.append(group_shift(rows, *n))
    grad_rows = list(gather_rows(owners[:1], ranks, held, local_clusters, capacity)) + grad_rows
    query_rows = own_rows(
        group.reshape(1),
        jnp.stack(sources),
        [SHARED] * len(near),
        owner_slots,
        query_all,
        token_count,
        local_clusters,
        capacity,
    )
    partials = block_grads(
        counts.reshape(local_clusters), query_rows, grad_rows, cluster_keys, values, capacity
    )
    returned = [partials[0]] + [
        group_shift(p, *[-n for n in steps]) for p, steps in zip(partials[1:], NEAR)
    ]
    partners = [0, *(core * (p[1] - p[0]) + p[0] for p in (FIRST, SECOND)), SHARED // 2]
    blocks = jnp.stack([group // apart ^ p for p in partners])
    mine, pair, kept = scatter_rows(owners, blocks, ranks, returned, capacity)
    came = partner_swap(pair, FIRST).astype(F32)
    last = partner_swap((kept + came[1]).astype(BF16), SECOND).astype(F32)
    return (mine + came[0] + last).astype(BF16)


def solution(mesh):
    placed = (
        P("grp", "pb"),
        P("grp", "pb"),
        P("grp", "pb"),
        P("pb", None),
        P("grp", "pb"),
        P("pb", "grp", None),
        P("pb", None),
        P("pb", "grp"),
        P("pb", "grp", None, None),
        P("pb", "grp", None, None),
    )
    return jax.shard_map(
        shards, mesh=mesh, in_specs=placed, out_specs=P("grp", "pb"), check_vma=False
    )
```

```python
import functools

import jax
import jax.numpy as jnp
from jax import lax
from jax.experimental import pallas as pl
from jax.experimental.pallas import tpu as pltpu
from jax.sharding import PartitionSpec as P

F32 = jnp.float32
BF16 = jnp.bfloat16
EXTRA = 8
NT = (((1,), (1,)), ((), ()))
TN = (((0,), (0,)), ((), ()))
SIDE, CORES = 4, 2
TURNS = (1, 3, 2)
SHARED = 4
FIRST, SECOND = (1, 3), (3, 1)
NEAR = ((1, 1), (-1, -1), (2, -2))
VMEM_BYTES = 48 * 1024 * 1024


def params():
    return pltpu.CompilerParams(vmem_limit_bytes=VMEM_BYTES)


def split_rows(row):
    high = row.astype(BF16).astype(F32)
    rest = row - high
    middle = rest.astype(BF16).astype(F32)
    low = (rest - middle).astype(BF16).astype(F32)
    return [high, middle, low]


def store_extra(out_ref, extra, tokens):
    for i in range(0, tokens // 128, 2):
        both = [extra[:, (i + k) * 128 : (i + k + 1) * 128] for k in range(2)]
        start = tokens + i * EXTRA
        out_ref[start : start + 2 * EXTRA, :] = jnp.concatenate(both, axis=0).astype(BF16)


def probe_rows(packed, tokens):
    packed, pieces = packed.astype(F32), tokens // 128
    return [
        jnp.concatenate([packed[j + i : j + i + 1] for i in range(pieces)], axis=1)
        for j in range(0, packed.shape[0], pieces)
    ]


def earlier_tokens(tokens):
    earlier = lax.broadcasted_iota(jnp.int32, (tokens, tokens), 0)
    later = lax.broadcasted_iota(jnp.int32, (tokens, tokens), 1)
    return jnp.where(earlier < later, 1.0, 0.0).astype(BF16)


def rank_kernel(table_ref, payload_ref, ranks_ref):
    blocks, clusters, tokens = ranks_ref.shape
    cluster = lax.broadcasted_iota(jnp.int32, (clusters, tokens), 0).astype(F32)
    slot = lax.broadcasted_iota(jnp.int32, (clusters, clusters), 0)
    table = jnp.where(table_ref[...] == slot, 1.0, 0.0).astype(BF16)
    before = earlier_tokens(tokens)
    start = tokens + EXTRA * tokens // 128
    for b in range(blocks):
        named = jnp.zeros((clusters, tokens), F32)
        for row in probe_rows(payload_ref[b, start:, :], tokens):
            named += jnp.where(row == cluster, 1.0, 0.0)
        marked = jnp.dot(table, named.astype(BF16), preferred_element_type=F32)
        ranking = jnp.dot(marked.astype(BF16), before, preferred_element_type=F32)
        ranks_ref[b] = jnp.where(marked > 0.5, ranking, -1.0)


def rank_slots(payloads, table, tokens):
    return pl.pallas_call(
        rank_kernel,
        out_shape=jax.ShapeDtypeStruct((payloads.shape[0], table.shape[1], tokens), F32),
        compiler_params=params(),
    )(table, payloads)


def weight_kernel(core_ref, weight_ref, own_ref, other_ref):
    pieces, _, piece = own_ref.shape
    core = core_ref[0]
    for i in range(pieces):
        for ref, side in ((own_ref, core), (other_ref, 1 - core)):
            start = pl.multiple_of((2 * i + side) * piece, piece)
            ref[i] = weight_ref[:, pl.ds(start, piece)]


def split_weight(core, weight, piece):
    width, depth = weight.shape
    half = jax.ShapeDtypeStruct((depth // piece // 2, width, piece), BF16)
    return pl.pallas_call(
        weight_kernel,
        in_specs=[
            pl.BlockSpec(memory_space=pltpu.SMEM),
            pl.BlockSpec(memory_space=pltpu.VMEM),
        ],
        out_shape=[half, half],
        compiler_params=params(),
    )(core, weight)


def product_kernel(turn, order_ref, own_ref, other_ref, *refs):
    halves, sums, results = refs[:2], refs[2:-2], refs[-2:]
    rows = halves[0].shape[1]
    for half, ref in enumerate(halves):
        span = slice(half * rows, (half + 1) * rows)
        total = None
        for m in range(ref.shape[0]):
            shard = order_ref[turn * ref.shape[0] + m]
            both = jnp.concatenate([own_ref[shard], other_ref[shard]], axis=0)
            term = lax.dot_general(ref[m], both, NT, preferred_element_type=F32)
            total = term if total is None else total + term
        width = total.shape[1] // 2
        for i, out_ref in enumerate(results):
            part = total[:, i * width : (i + 1) * width]
            out_ref[span, :] = part + sums[i][span, :] if sums else part


def partial_product(turn, order, own, other, halves, sums):
    result = jax.ShapeDtypeStruct((2 * halves[0].shape[1], own.shape[1]), F32)
    return pl.pallas_call(
        functools.partial(product_kernel, turn),
        in_specs=[pl.BlockSpec(memory_space=pltpu.SMEM)]
        + [pl.BlockSpec(memory_space=pltpu.VMEM)] * (4 + len(sums)),
        out_shape=[result, result],
        compiler_params=params(),
    )(order, own, other, *halves, *sums)


def grad_kernel(own_ref, other_ref, outputs_ref, norm_ref, packed_ref, out_ref):
    tokens = outputs_ref.shape[0]
    grad = (own_ref[...] + other_ref[...]).astype(BF16)
    out_ref[0:tokens, :] = grad
    product = grad.astype(F32) * outputs_ref[...].astype(F32)
    delta = jnp.sum(product.T, axis=0, keepdims=True)
    sides = split_rows(delta) + split_rows(norm_ref[...])
    sides.append(jnp.zeros((EXTRA - len(sides), tokens), F32))
    store_extra(out_ref, jnp.concatenate(sides, axis=0), tokens)
    out_ref[tokens + EXTRA * tokens // 128 :, :] = packed_ref[...]


def grad_payload(own, other, outputs, norm_row, packed):
    tokens, width = outputs.shape
    rows = tokens + EXTRA * tokens // 128 + packed.shape[0]
    return pl.pallas_call(
        grad_kernel,
        out_shape=jax.ShapeDtypeStruct((rows, width), BF16),
        compiler_params=params(),
    )(own, other, outputs, norm_row, packed)


def choices(ranks, capacity):
    slots, tokens = ranks.shape
    place = lax.broadcasted_iota(jnp.int32, (capacity, tokens), 0).astype(F32)
    rows = [jnp.where(ranks[s : s + 1, :] == place, 1.0, 0.0) for s in range(slots)]
    return jnp.concatenate(rows, axis=0).astype(BF16)


def owner_ranks(ranks_ref, block, owner, local_clusters):
    start = pl.multiple_of(owner * local_clusters, local_clusters)
    return ranks_ref[block, pl.ds(start, local_clusters), :]


def pick_rows(payload_ref, chosen, tokens, out_ref):
    picked = chosen.shape[0]
    parts = [
        payload_ref[tokens + i * 2 * EXTRA : tokens + (i + 1) * 2 * EXTRA, :].astype(F32)
        for i in range(tokens // 256)
    ]
    wide = [part[k * EXTRA : (k + 1) * EXTRA] for part in parts for k in range(2)]
    extra = jnp.concatenate(wide, axis=1).astype(BF16)
    out_ref[0:picked, :] = jnp.dot(
        chosen, payload_ref[0:tokens, :], preferred_element_type=F32
    ).astype(BF16)
    moved = lax.dot_general(extra, chosen, NT, preferred_element_type=F32)
    both = [moved[:, k * 128 : (k + 1) * 128] for k in range(picked // 128)]
    out_ref[picked:, :] = jnp.concatenate(both, axis=0).astype(BF16)


def gather_kernel(capacity, local_clusters, owners_ref, ranks_ref, payload_ref, *refs):
    blocks, _, tokens = ranks_ref.shape
    for b in range(blocks):
        for i, out_ref in enumerate(refs):
            chosen = choices(
                owner_ranks(ranks_ref, b, owners_ref[i], local_clusters), capacity
            )
            pick_rows(payload_ref.at[b], chosen, tokens, out_ref.at[b])


def gather_rows(owners, ranks, payloads, local_clusters, capacity):
    blocks, width = ranks.shape[0], payloads.shape[-1]
    picked = local_clusters * capacity
    rows = jax.ShapeDtypeStruct((blocks, picked + EXTRA * picked // 128, width), BF16)
    return pl.pallas_call(
        functools.partial(gather_kernel, capacity, local_clusters),
        in_specs=[pl.BlockSpec(memory_space=pltpu.SMEM)]
        + [pl.BlockSpec(memory_space=pltpu.VMEM)] * 2,
        out_shape=[rows] * owners.shape[0],
        compiler_params=params(),
    )(owners, ranks, payloads)


def own_kernel(capacity, tokens, group_ref, sources_ref, table_ref, payload_ref, *refs):
    places = [(i, b) for i, ref in enumerate(refs) for b in range(ref.shape[0])]
    local_clusters = refs[0].shape[1] // capacity
    clusters = table_ref.shape[1]
    slot = lax.broadcasted_iota(jnp.int32, (local_clusters, clusters), 0)
    cluster = lax.broadcasted_iota(jnp.int32, (local_clusters, clusters), 1)
    mine = table_ref[...] == slot + group_ref[0] * local_clusters
    stored = jnp.sum(jnp.where(mine, cluster.astype(F32), 0.0), axis=1, keepdims=True)
    marks = []
    for k in range(len(places)):
        named = jnp.zeros((local_clusters, tokens), F32)
        for row in probe_rows(payload_ref[sources_ref[k], tokens:, :], tokens):
            named += jnp.where(row == stored, 1.0, 0.0)
        marks.append(named)
    marks = jnp.concatenate(marks, axis=0)
    ranking = jnp.dot(marks.astype(BF16), earlier_tokens(tokens), preferred_element_type=F32)
    ranks = jnp.where(marks > 0.5, ranking, -1.0)
    for k, (i, b) in enumerate(places):
        chosen = choices(ranks[k * local_clusters : (k + 1) * local_clusters], capacity)
        rows = payload_ref[sources_ref[k], 0:tokens, :]
        refs[i][b] = jnp.dot(chosen, rows, preferred_element_type=F32).astype(BF16)


def own_rows(group, sources, counts, table, payloads, tokens, local_clusters, capacity):
    picked = local_clusters * capacity
    width = payloads.shape[-1]
    rows = [(count, picked, width) for count in counts]
    return pl.pallas_call(
        functools.partial(own_kernel, capacity, tokens),
        in_specs=[pl.BlockSpec(memory_space=pltpu.SMEM)] * 2
        + [pl.BlockSpec(memory_space=pltpu.VMEM)] * 2,
        out_shape=[jax.ShapeDtypeStruct(shape, BF16) for shape in rows],
        compiler_params=params(),
    )(group, sources, table, payloads)


def scatter_kernel(capacity, owners_ref, held_ref, ranks_ref, *refs):
    partial_refs, places = refs[:-4], refs[-4:]
    local_clusters = partial_refs[0].shape[1] // capacity
    for k in (3, 1, 2, 0):
        b = held_ref[k]
        total = None
        for i, partial_ref in enumerate(partial_refs):
            chosen = choices(
                owner_ranks(ranks_ref, b, owners_ref[i], local_clusters), capacity
            )
            term = lax.dot_general(partial_ref[b], chosen, TN, preferred_element_type=F32)
            total = term if total is None else total + term
        places[k][...] = total.T.astype(places[k].dtype)


def scatter_rows(owners, held, ranks, partials, capacity):
    tokens, width = ranks.shape[2], partials[0].shape[2]
    return pl.pallas_call(
        functools.partial(scatter_kernel, capacity),
        in_specs=[pl.BlockSpec(memory_space=pltpu.SMEM)] * 2
        + [pl.BlockSpec(memory_space=pltpu.VMEM)] * (1 + len(partials)),
        out_shape=[
            jax.ShapeDtypeStruct((tokens, width), kind) for kind in (F32, BF16, F32, BF16)
        ],
        compiler_params=params(),
    )(owners, held, ranks, *partials)


def unpack_extra(extra_refs, delta_ref, norm_ref, capacity):
    places = [(i, b) for i, ref in enumerate(extra_refs) for b in range(ref.shape[0])]
    per_row = 128 // capacity
    lane = lax.broadcasted_iota(jnp.int32, (2 * EXTRA, 128), 1) // capacity
    for sub in range(per_row):
        for group in range(len(places) // per_row):
            total = jnp.zeros((2 * EXTRA, 128), F32)
            for k in range(per_row):
                side, sender = places[group * per_row + k]
                packed = extra_refs[side][sender].astype(F32)
                turn = (k - sub) * capacity % 128
                if turn:
                    packed = pltpu.roll(packed, turn, 1)
                total += jnp.where(lane == k, packed, 0.0)
            lanes = slice(group * 128, (group + 1) * 128)
            for half in range(2):
                cluster = half * per_row + sub
                for start, ref in ((half * EXTRA, delta_ref), (half * EXTRA + 3, norm_ref)):
                    rows = [total[start + i : start + i + 1] for i in range(3)]
                    ref[cluster : cluster + 1, lanes] = rows[0] + rows[1] + rows[2]


def block_kernel(capacity, sides, counts_ref, *refs):
    query_refs, grad_refs = refs[:sides], refs[sides : 2 * sides]
    key_ref, value_ref = refs[2 * sides : 2 * sides + 2]
    out_refs = refs[2 * sides + 2 : 3 * sides + 2]
    norm_ref, delta_ref = refs[3 * sides + 2 :]
    width = query_refs[0].shape[2]
    local_clusters, span = key_ref.shape[1:3]
    score_scale = width ** (-0.5)
    arrivals = norm_ref.shape[1]
    behind = slice(local_clusters * capacity, local_clusters * capacity + 2 * EXTRA)
    unpack_extra([ref.at[:, behind, :] for ref in grad_refs], delta_ref, norm_ref, capacity)
    place = lax.broadcasted_iota(jnp.int32, (span, arrivals), 0)

    for c in range(local_clusters):
        mine = slice(c * capacity, (c + 1) * capacity)
        query, grad = (
            jnp.concatenate([ref[:, mine, :].reshape(-1, width) for ref in side], axis=0)
            for side in (query_refs, grad_refs)
        )
        keys = key_ref[0, c]
        scores = lax.dot_general(keys, query, NT, preferred_element_type=F32) * score_scale
        weights = jnp.where(
            place < counts_ref[c], jnp.exp(scores - norm_ref[c : c + 1, :]), 0.0
        )
        grad_prob = lax.dot_general(value_ref[0, c], grad, NT, preferred_element_type=F32)
        grad_score = (weights * (grad_prob - delta_ref[c : c + 1, :])).astype(BF16)
        partial = lax.dot_general(keys, grad_score, TN, preferred_element_type=F32)
        partial = (partial * score_scale).T.astype(BF16)
        start = 0
        for out_ref in out_refs:
            stop = start + out_ref.shape[0] * capacity
            out_ref[:, mine, :] = partial[start:stop].reshape(-1, capacity, width)
            start = stop


def block_grads(counts, query_rows, grad_rows, keys, values, capacity):
    sides = len(query_rows)
    width = query_rows[0].shape[2]
    local_clusters = keys.shape[1]
    picked = local_clusters * capacity
    senders = [rows.shape[0] for rows in query_rows]
    arrivals = sum(senders) * capacity
    return pl.pallas_call(
        functools.partial(block_kernel, capacity, sides),
        in_specs=[pl.BlockSpec(memory_space=pltpu.SMEM)]
        + [pl.BlockSpec(memory_space=pltpu.VMEM)] * (2 * sides + 2),
        out_shape=[jax.ShapeDtypeStruct((count, picked, width), BF16) for count in senders],
        scratch_shapes=[pltpu.VMEM((local_clusters, arrivals), F32)] * 2,
        compiler_params=params(),
    )(counts, *query_rows, *grad_rows, keys, values)


def plane_shift(array, turn, phase):
    pairs = []
    for x in range(SIDE):
        for y in range(SIDE):
            for core in range(CORES):
                across, along = (turn, 0) if core == phase else (0, turn)
                target = (x + across) % SIDE * SIDE + (y + along) % SIDE
                pairs.append(((x * SIDE + y) * CORES + core, target * CORES + core))
    return lax.ppermute(array, "pb", pairs)


def swap_cores(array):
    return lax.ppermute(array, "pb", [(i, i ^ 1) for i in range(SIDE * SIDE * CORES)])


def group_shift(array, *steps):
    groups, width = lax.axis_size("grp"), lax.axis_size("pb")
    pairs = [
        (g * width + p, (g + steps[p % len(steps)]) % groups * width + p)
        for g in range(groups)
        for p in range(width)
    ]
    return lax.ppermute(array, ("grp", "pb"), pairs)


def partner_swap(array, partner):
    groups, width = lax.axis_size("grp"), lax.axis_size("pb")
    apart = groups // SHARED
    pairs = [
        (g * width + p, (g ^ (partner[p % CORES] * apart)) * width + p)
        for g in range(groups)
        for p in range(width)
    ]
    return lax.ppermute(array, ("grp", "pb"), pairs)


def shards(
    queries,
    outputs,
    readout_grad,
    readout_weight,
    log_norm,
    probes,
    owner_slots,
    counts,
    cluster_keys,
    values,
):
    token_count = queries.shape[0]
    probe_count = probes.shape[2]
    local_clusters = cluster_keys.shape[1]
    clusters = owner_slots.shape[1]
    capacity = 2 * token_count * probe_count // clusters
    groups = lax.axis_size("grp")
    group, place = lax.axis_index("grp"), lax.axis_index("pb")
    core, column, line = place % CORES, place // (CORES * SIDE), place // CORES % SIDE
    apart = groups // SHARED
    sets = [[g + apart * i for i in range(SHARED)] for g in range(apart)]
    near = [0, 1, -1, 2 - 4 * core]
    owners = jnp.stack([(group + n) % groups for n in near])
    sources = [(group - n) % groups % apart + apart * b for n in near for b in range(SHARED)]

    packed = probes[0].T.reshape(-1, 128).astype(BF16)
    query_all = lax.all_gather(jnp.concatenate([queries, packed], axis=0), "grp")

    piece = readout_grad.shape[1]
    first = [readout_grad] + [plane_shift(readout_grad, d, 0) for d in TURNS]
    half = token_count // 2
    upper = jnp.stack([p[:half] for p in first])
    lower = jnp.stack([p[half:] for p in first])
    own, other = split_weight(core.reshape(1), readout_weight, piece)
    other = swap_cores(other)
    before_up, after_low = plane_shift(upper, 1, 1), plane_shift(lower, -1, 1)
    before_low, after_up = plane_shift(lower, 1, 1), plane_shift(upper, -1, 1)
    far_up, far_low = plane_shift(before_up, 1, 1), plane_shift(after_low, -1, 1)
    turns = jnp.asarray((0,) + TURNS, jnp.int32)
    xs, ys = (column - turns) % SIDE, (line - turns) % SIDE
    order = jnp.where(
        core == 0,
        xs[None, :] * SIDE + ys[:, None],
        xs[:, None] * SIDE + ys[None, :],
    ).reshape(-1)
    arrivals = [(upper, lower), (before_up, before_low), (after_up, after_low), (far_up, far_low)]
    sums = []
    for turn, halves in enumerate(arrivals):
        sums = partial_product(turn, order, own, other, halves, sums)
    norm_row = log_norm.reshape(1, token_count)
    payload = grad_payload(sums[0], swap_cores(sums[1]), outputs, norm_row, packed)
    held = lax.all_gather(payload, "grp", axis_index_groups=sets)
    ranks = rank_slots(held, owner_slots, token_count)
    grad_rows = []
    for i, n in enumerate(NEAR):
        (rows,) = gather_rows(owners[i + 1 : i + 2], ranks, held, local_clusters, capacity)
        grad_rows.append(group_shift(rows, *n))
    grad_rows = list(gather_rows(owners[:1], ranks, held, local_clusters, capacity)) + grad_rows
    query_rows = own_rows(
        group.reshape(1),
        jnp.stack(sources),
        [SHARED] * len(near),
        owner_slots,
        query_all,
        token_count,
        local_clusters,
        capacity,
    )
    partials = block_grads(
        counts.reshape(local_clusters), query_rows, grad_rows, cluster_keys, values, capacity
    )
    returned = [partials[0]] + [
        group_shift(p, *[-n for n in steps]) for p, steps in zip(partials[1:], NEAR)
    ]
    partners = [0, *(core * (p[1] - p[0]) + p[0] for p in (FIRST, SECOND)), SHARED // 2]
    blocks = jnp.stack([group // apart ^ p for p in partners])
    mine, near_by, kept, passed = scatter_rows(owners, blocks, ranks, returned, capacity)
    kept = kept + partner_swap(passed, FIRST).astype(F32)
    came = partner_swap(near_by, FIRST).astype(F32)
    last = partner_swap(kept.astype(BF16), SECOND).astype(F32)
    return (mine + came + last).astype(BF16)


def solution(mesh):
    placed = (
        P("grp", "pb"),
        P("grp", "pb"),
        P("grp", "pb"),
        P("pb", None),
        P("grp", "pb"),
        P("pb", "grp", None),
        P("pb", None),
        P("pb", "grp"),
        P("pb", "grp", None, None),
        P("pb", "grp", None, None),
    )
    return jax.shard_map(
        shards, mesh=mesh, in_specs=placed, out_specs=P("grp", "pb"), check_vma=False
    )
```

```python
import functools

import jax
import jax.numpy as jnp
from jax import lax
from jax.experimental import pallas as pl
from jax.experimental.pallas import tpu as pltpu
from jax.sharding import PartitionSpec as P

F32 = jnp.float32
BF16 = jnp.bfloat16
EXTRA = 8
NT = (((1,), (1,)), ((), ()))
TN = (((0,), (0,)), ((), ()))
SIDE, CORES = 4, 2
TURNS = (1, 3, 2)
SHARED = 4
FIRST, SECOND = (1, 3), (3, 1)
NEAR = ((1, -1), (-1, 1), (2, -2))
VMEM_BYTES = 48 * 1024 * 1024


def params():
    return pltpu.CompilerParams(vmem_limit_bytes=VMEM_BYTES)


def split_rows(row):
    high = row.astype(BF16).astype(F32)
    rest = row - high
    middle = rest.astype(BF16).astype(F32)
    low = (rest - middle).astype(BF16).astype(F32)
    return [high, middle, low]


def store_extra(out_ref, extra, tokens):
    for i in range(0, tokens // 128, 2):
        both = [extra[:, (i + k) * 128 : (i + k + 1) * 128] for k in range(2)]
        start = tokens + i * EXTRA
        out_ref[start : start + 2 * EXTRA, :] = jnp.concatenate(both, axis=0).astype(BF16)


def probe_rows(packed, tokens):
    packed, pieces = packed.astype(F32), tokens // 128
    return [
        jnp.concatenate([packed[j + i : j + i + 1] for i in range(pieces)], axis=1)
        for j in range(0, packed.shape[0], pieces)
    ]


def earlier_tokens(tokens):
    earlier = lax.broadcasted_iota(jnp.int32, (tokens, tokens), 0)
    later = lax.broadcasted_iota(jnp.int32, (tokens, tokens), 1)
    return jnp.where(earlier < later, 1.0, 0.0).astype(BF16)


def rank_kernel(table_ref, payload_ref, ranks_ref):
    blocks, clusters, tokens = ranks_ref.shape
    cluster = lax.broadcasted_iota(jnp.int32, (clusters, tokens), 0).astype(F32)
    slot = lax.broadcasted_iota(jnp.int32, (clusters, clusters), 0)
    table = jnp.where(table_ref[...] == slot, 1.0, 0.0).astype(BF16)
    before = earlier_tokens(tokens)
    start = tokens + EXTRA * tokens // 128
    for b in range(blocks):
        named = jnp.zeros((clusters, tokens), F32)
        for row in probe_rows(payload_ref[b, start:, :], tokens):
            named += jnp.where(row == cluster, 1.0, 0.0)
        marked = jnp.dot(table, named.astype(BF16), preferred_element_type=F32)
        ranking = jnp.dot(marked.astype(BF16), before, preferred_element_type=F32)
        ranks_ref[b] = jnp.where(marked > 0.5, ranking, -1.0)


def rank_slots(payloads, table, tokens):
    return pl.pallas_call(
        rank_kernel,
        out_shape=jax.ShapeDtypeStruct((payloads.shape[0], table.shape[1], tokens), F32),
        compiler_params=params(),
    )(table, payloads)


def weight_kernel(core_ref, weight_ref, own_ref, other_ref):
    pieces, _, piece = own_ref.shape
    core = core_ref[0]
    for i in range(pieces):
        for ref, side in ((own_ref, core), (other_ref, 1 - core)):
            start = pl.multiple_of((2 * i + side) * piece, piece)
            ref[i] = weight_ref[:, pl.ds(start, piece)]


def split_weight(core, weight, piece):
    width, depth = weight.shape
    half = jax.ShapeDtypeStruct((depth // piece // 2, width, piece), BF16)
    return pl.pallas_call(
        weight_kernel,
        in_specs=[
            pl.BlockSpec(memory_space=pltpu.SMEM),
            pl.BlockSpec(memory_space=pltpu.VMEM),
        ],
        out_shape=[half, half],
        compiler_params=params(),
    )(core, weight)


def product_kernel(turn, order_ref, own_ref, other_ref, *refs):
    halves, sums, results = refs[:2], refs[2:-2], refs[-2:]
    rows = halves[0].shape[1]
    for half, ref in enumerate(halves):
        span = slice(half * rows, (half + 1) * rows)
        total = None
        for m in range(ref.shape[0]):
            shard = order_ref[turn * ref.shape[0] + m]
            both = jnp.concatenate([own_ref[shard], other_ref[shard]], axis=0)
            term = lax.dot_general(ref[m], both, NT, preferred_element_type=F32)
            total = term if total is None else total + term
        width = total.shape[1] // 2
        for i, out_ref in enumerate(results):
            part = total[:, i * width : (i + 1) * width]
            out_ref[span, :] = part + sums[i][span, :] if sums else part


def partial_product(turn, order, own, other, halves, sums):
    result = jax.ShapeDtypeStruct((2 * halves[0].shape[1], own.shape[1]), F32)
    return pl.pallas_call(
        functools.partial(product_kernel, turn),
        in_specs=[pl.BlockSpec(memory_space=pltpu.SMEM)]
        + [pl.BlockSpec(memory_space=pltpu.VMEM)] * (4 + len(sums)),
        out_shape=[result, result],
        compiler_params=params(),
    )(order, own, other, *halves, *sums)


def grad_kernel(own_ref, other_ref, outputs_ref, norm_ref, packed_ref, out_ref):
    tokens = outputs_ref.shape[0]
    grad = (own_ref[...] + other_ref[...]).astype(BF16)
    out_ref[0:tokens, :] = grad
    product = grad.astype(F32) * outputs_ref[...].astype(F32)
    delta = jnp.sum(product.T, axis=0, keepdims=True)
    sides = split_rows(delta) + split_rows(norm_ref[...])
    sides.append(jnp.zeros((EXTRA - len(sides), tokens), F32))
    store_extra(out_ref, jnp.concatenate(sides, axis=0), tokens)
    out_ref[tokens + EXTRA * tokens // 128 :, :] = packed_ref[...]


def grad_payload(own, other, outputs, norm_row, packed):
    tokens, width = outputs.shape
    rows = tokens + EXTRA * tokens // 128 + packed.shape[0]
    return pl.pallas_call(
        grad_kernel,
        out_shape=jax.ShapeDtypeStruct((rows, width), BF16),
        compiler_params=params(),
    )(own, other, outputs, norm_row, packed)


def choices(ranks, capacity):
    slots, tokens = ranks.shape
    place = lax.broadcasted_iota(jnp.int32, (capacity, tokens), 0).astype(F32)
    rows = [jnp.where(ranks[s : s + 1, :] == place, 1.0, 0.0) for s in range(slots)]
    return jnp.concatenate(rows, axis=0).astype(BF16)


def owner_ranks(ranks_ref, block, owner, local_clusters):
    start = pl.multiple_of(owner * local_clusters, local_clusters)
    return ranks_ref[block, pl.ds(start, local_clusters), :]


def pick_rows(payload_ref, chosen, tokens, out_ref):
    picked = chosen.shape[0]
    parts = [
        payload_ref[tokens + i * 2 * EXTRA : tokens + (i + 1) * 2 * EXTRA, :].astype(F32)
        for i in range(tokens // 256)
    ]
    wide = [part[k * EXTRA : (k + 1) * EXTRA] for part in parts for k in range(2)]
    extra = jnp.concatenate(wide, axis=1).astype(BF16)
    out_ref[0:picked, :] = jnp.dot(
        chosen, payload_ref[0:tokens, :], preferred_element_type=F32
    ).astype(BF16)
    moved = lax.dot_general(extra, chosen, NT, preferred_element_type=F32)
    both = [moved[:, k * 128 : (k + 1) * 128] for k in range(picked // 128)]
    out_ref[picked:, :] = jnp.concatenate(both, axis=0).astype(BF16)


def gather_kernel(capacity, local_clusters, owners_ref, ranks_ref, payload_ref, *refs):
    blocks, _, tokens = ranks_ref.shape
    for b in range(blocks):
        for i, out_ref in enumerate(refs):
            chosen = choices(
                owner_ranks(ranks_ref, b, owners_ref[i], local_clusters), capacity
            )
            pick_rows(payload_ref.at[b], chosen, tokens, out_ref.at[b])


def gather_rows(owners, ranks, payloads, local_clusters, capacity):
    blocks, width = ranks.shape[0], payloads.shape[-1]
    picked = local_clusters * capacity
    rows = jax.ShapeDtypeStruct((blocks, picked + EXTRA * picked // 128, width), BF16)
    return pl.pallas_call(
        functools.partial(gather_kernel, capacity, local_clusters),
        in_specs=[pl.BlockSpec(memory_space=pltpu.SMEM)]
        + [pl.BlockSpec(memory_space=pltpu.VMEM)] * 2,
        out_shape=[rows] * owners.shape[0],
        compiler_params=params(),
    )(owners, ranks, payloads)


def own_kernel(capacity, tokens, group_ref, sources_ref, table_ref, payload_ref, *refs):
    places = [(i, b) for i, ref in enumerate(refs) for b in range(ref.shape[0])]
    local_clusters = refs[0].shape[1] // capacity
    clusters = table_ref.shape[1]
    slot = lax.broadcasted_iota(jnp.int32, (local_clusters, clusters), 0)
    cluster = lax.broadcasted_iota(jnp.int32, (local_clusters, clusters), 1)
    mine = table_ref[...] == slot + group_ref[0] * local_clusters
    stored = jnp.sum(jnp.where(mine, cluster.astype(F32), 0.0), axis=1, keepdims=True)
    marks = []
    for k in range(len(places)):
        named = jnp.zeros((local_clusters, tokens), F32)
        for row in probe_rows(payload_ref[sources_ref[k], tokens:, :], tokens):
            named += jnp.where(row == stored, 1.0, 0.0)
        marks.append(named)
    marks = jnp.concatenate(marks, axis=0)
    ranking = jnp.dot(marks.astype(BF16), earlier_tokens(tokens), preferred_element_type=F32)
    ranks = jnp.where(marks > 0.5, ranking, -1.0)
    for k, (i, b) in enumerate(places):
        chosen = choices(ranks[k * local_clusters : (k + 1) * local_clusters], capacity)
        rows = payload_ref[sources_ref[k], 0:tokens, :]
        refs[i][b] = jnp.dot(chosen, rows, preferred_element_type=F32).astype(BF16)


def own_rows(group, sources, counts, table, payloads, tokens, local_clusters, capacity):
    picked = local_clusters * capacity
    width = payloads.shape[-1]
    rows = [(count, picked, width) for count in counts]
    return pl.pallas_call(
        functools.partial(own_kernel, capacity, tokens),
        in_specs=[pl.BlockSpec(memory_space=pltpu.SMEM)] * 2
        + [pl.BlockSpec(memory_space=pltpu.VMEM)] * 2,
        out_shape=[jax.ShapeDtypeStruct(shape, BF16) for shape in rows],
        compiler_params=params(),
    )(group, sources, table, payloads)


def scatter_kernel(capacity, owners_ref, held_ref, ranks_ref, *refs):
    partial_refs, places = refs[:-4], refs[-4:]
    local_clusters = partial_refs[0].shape[1] // capacity
    for k in (3, 1, 2, 0):
        b = held_ref[k]
        total = None
        for i, partial_ref in enumerate(partial_refs):
            chosen = choices(
                owner_ranks(ranks_ref, b, owners_ref[i], local_clusters), capacity
            )
            term = lax.dot_general(partial_ref[b], chosen, TN, preferred_element_type=F32)
            total = term if total is None else total + term
        places[k][...] = total.T.astype(places[k].dtype)


def scatter_rows(owners, held, ranks, partials, capacity):
    tokens, width = ranks.shape[2], partials[0].shape[2]
    return pl.pallas_call(
        functools.partial(scatter_kernel, capacity),
        in_specs=[pl.BlockSpec(memory_space=pltpu.SMEM)] * 2
        + [pl.BlockSpec(memory_space=pltpu.VMEM)] * (1 + len(partials)),
        out_shape=[
            jax.ShapeDtypeStruct((tokens, width), kind) for kind in (F32, BF16, F32, BF16)
        ],
        compiler_params=params(),
    )(owners, held, ranks, *partials)


def unpack_extra(extra_refs, delta_ref, norm_ref, capacity):
    places = [(i, b) for i, ref in enumerate(extra_refs) for b in range(ref.shape[0])]
    per_row = 128 // capacity
    lane = lax.broadcasted_iota(jnp.int32, (2 * EXTRA, 128), 1) // capacity
    for sub in range(per_row):
        for group in range(len(places) // per_row):
            total = jnp.zeros((2 * EXTRA, 128), F32)
            for k in range(per_row):
                side, sender = places[group * per_row + k]
                packed = extra_refs[side][sender].astype(F32)
                turn = (k - sub) * capacity % 128
                if turn:
                    packed = pltpu.roll(packed, turn, 1)
                total += jnp.where(lane == k, packed, 0.0)
            lanes = slice(group * 128, (group + 1) * 128)
            for half in range(2):
                cluster = half * per_row + sub
                for start, ref in ((half * EXTRA, delta_ref), (half * EXTRA + 3, norm_ref)):
                    rows = [total[start + i : start + i + 1] for i in range(3)]
                    ref[cluster : cluster + 1, lanes] = rows[0] + rows[1] + rows[2]


def block_kernel(capacity, sides, counts_ref, *refs):
    query_refs, grad_refs = refs[:sides], refs[sides : 2 * sides]
    key_ref, value_ref = refs[2 * sides : 2 * sides + 2]
    out_refs = refs[2 * sides + 2 : 3 * sides + 2]
    norm_ref, delta_ref = refs[3 * sides + 2 :]
    width = query_refs[0].shape[2]
    local_clusters, span = key_ref.shape[1:3]
    score_scale = width ** (-0.5)
    arrivals = norm_ref.shape[1]
    behind = slice(local_clusters * capacity, local_clusters * capacity + 2 * EXTRA)
    unpack_extra([ref.at[:, behind, :] for ref in grad_refs], delta_ref, norm_ref, capacity)
    place = lax.broadcasted_iota(jnp.int32, (span, arrivals), 0)

    for c in range(local_clusters):
        mine = slice(c * capacity, (c + 1) * capacity)
        query, grad = (
            jnp.concatenate([ref[:, mine, :].reshape(-1, width) for ref in side], axis=0)
            for side in (query_refs, grad_refs)
        )
        keys = key_ref[0, c]
        scores = lax.dot_general(keys, query, NT, preferred_element_type=F32) * score_scale
        weights = jnp.where(
            place < counts_ref[c], jnp.exp(scores - norm_ref[c : c + 1, :]), 0.0
        )
        grad_prob = lax.dot_general(value_ref[0, c], grad, NT, preferred_element_type=F32)
        grad_score = (weights * (grad_prob - delta_ref[c : c + 1, :])).astype(BF16)
        partial = lax.dot_general(keys, grad_score, TN, preferred_element_type=F32)
        partial = (partial * score_scale).T.astype(BF16)
        start = 0
        for out_ref in out_refs:
            stop = start + out_ref.shape[0] * capacity
            out_ref[:, mine, :] = partial[start:stop].reshape(-1, capacity, width)
            start = stop


def block_grads(counts, query_rows, grad_rows, keys, values, capacity):
    sides = len(query_rows)
    width = query_rows[0].shape[2]
    local_clusters = keys.shape[1]
    picked = local_clusters * capacity
    senders = [rows.shape[0] for rows in query_rows]
    arrivals = sum(senders) * capacity
    return pl.pallas_call(
        functools.partial(block_kernel, capacity, sides),
        in_specs=[pl.BlockSpec(memory_space=pltpu.SMEM)]
        + [pl.BlockSpec(memory_space=pltpu.VMEM)] * (2 * sides + 2),
        out_shape=[jax.ShapeDtypeStruct((count, picked, width), BF16) for count in senders],
        scratch_shapes=[pltpu.VMEM((local_clusters, arrivals), F32)] * 2,
        compiler_params=params(),
    )(counts, *query_rows, *grad_rows, keys, values)


def plane_shift(array, turn, phase):
    pairs = []
    for x in range(SIDE):
        for y in range(SIDE):
            for core in range(CORES):
                across, along = (turn, 0) if core == phase else (0, turn)
                target = (x + across) % SIDE * SIDE + (y + along) % SIDE
                pairs.append(((x * SIDE + y) * CORES + core, target * CORES + core))
    return lax.ppermute(array, "pb", pairs)


def swap_cores(array):
    return lax.ppermute(array, "pb", [(i, i ^ 1) for i in range(SIDE * SIDE * CORES)])


def group_shift(array, *steps):
    groups, width = lax.axis_size("grp"), lax.axis_size("pb")
    pairs = [
        (g * width + p, (g + steps[p % len(steps)]) % groups * width + p)
        for g in range(groups)
        for p in range(width)
    ]
    return lax.ppermute(array, ("grp", "pb"), pairs)


def partner_swap(array, partner):
    groups, width = lax.axis_size("grp"), lax.axis_size("pb")
    apart = groups // SHARED
    pairs = [
        (g * width + p, (g ^ (partner[p % CORES] * apart)) * width + p)
        for g in range(groups)
        for p in range(width)
    ]
    return lax.ppermute(array, ("grp", "pb"), pairs)


def shards(
    queries,
    outputs,
    readout_grad,
    readout_weight,
    log_norm,
    probes,
    owner_slots,
    counts,
    cluster_keys,
    values,
):
    token_count = queries.shape[0]
    probe_count = probes.shape[2]
    local_clusters = cluster_keys.shape[1]
    clusters = owner_slots.shape[1]
    capacity = 2 * token_count * probe_count // clusters
    groups = lax.axis_size("grp")
    group, place = lax.axis_index("grp"), lax.axis_index("pb")
    core, column, line = place % CORES, place // (CORES * SIDE), place // CORES % SIDE
    apart = groups // SHARED
    sets = [[g + apart * i for i in range(SHARED)] for g in range(apart)]
    near = [0] + [core * (n[1] - n[0]) + n[0] for n in NEAR]
    owners = jnp.stack([(group + n) % groups for n in near])
    sources = [(group - n) % groups % apart + apart * b for n in near for b in range(SHARED)]

    packed = probes[0].T.reshape(-1, 128).astype(BF16)
    query_all = lax.all_gather(jnp.concatenate([queries, packed], axis=0), "grp")

    piece = readout_grad.shape[1]
    first = [readout_grad] + [plane_shift(readout_grad, d, 0) for d in TURNS]
    half = token_count // 2
    upper = jnp.stack([p[:half] for p in first])
    lower = jnp.stack([p[half:] for p in first])
    own, other = split_weight(core.reshape(1), readout_weight, piece)
    other = swap_cores(other)
    before_up, after_low = plane_shift(upper, 1, 1), plane_shift(lower, -1, 1)
    before_low, after_up = plane_shift(lower, 1, 1), plane_shift(upper, -1, 1)
    far_up, far_low = plane_shift(before_up, 1, 1), plane_shift(after_low, -1, 1)
    turns = jnp.asarray((0,) + TURNS, jnp.int32)
    xs, ys = (column - turns) % SIDE, (line - turns) % SIDE
    order = jnp.where(
        core == 0,
        xs[None, :] * SIDE + ys[:, None],
        xs[:, None] * SIDE + ys[None, :],
    ).reshape(-1)
    arrivals = [(upper, lower), (before_up, before_low), (after_up, after_low), (far_up, far_low)]
    sums = []
    for turn, halves in enumerate(arrivals):
        sums = partial_product(turn, order, own, other, halves, sums)
    norm_row = log_norm.reshape(1, token_count)
    payload = grad_payload(sums[0], swap_cores(sums[1]), outputs, norm_row, packed)
    held = lax.all_gather(payload, "grp", axis_index_groups=sets)
    ranks = rank_slots(held, owner_slots, token_count)
    grad_rows = []
    for i, n in enumerate(NEAR):
        (rows,) = gather_rows(owners[i + 1 : i + 2], ranks, held, local_clusters, capacity)
        grad_rows.append(group_shift(rows, *n))
    grad_rows = list(gather_rows(owners[:1], ranks, held, local_clusters, capacity)) + grad_rows
    query_rows = own_rows(
        group.reshape(1),
        jnp.stack(sources),
        [SHARED] * len(near),
        owner_slots,
        query_all,
        token_count,
        local_clusters,
        capacity,
    )
    partials = block_grads(
        counts.reshape(local_clusters), query_rows, grad_rows, cluster_keys, values, capacity
    )
    returned = [partials[0]] + [
        group_shift(p, *[-n for n in steps]) for p, steps in zip(partials[1:], NEAR)
    ]
    partners = [0, *(core * (p[1] - p[0]) + p[0] for p in (FIRST, SECOND)), SHARED // 2]
    blocks = jnp.stack([group // apart ^ p for p in partners])
    back = (0, 3, 1, 2)
    mine, near_by, kept, passed = scatter_rows(
        jnp.stack([owners[i] for i in back]), blocks, ranks, [returned[i] for i in back], capacity
    )
    kept = kept + partner_swap(passed, FIRST).astype(F32)
    came = partner_swap(near_by, FIRST).astype(F32)
    last = partner_swap(kept.astype(BF16), SECOND).astype(F32)
    return (mine + came + last).astype(BF16)


def solution(mesh):
    placed = (
        P("grp", "pb"),
        P("grp", "pb"),
        P("grp", "pb"),
        P("pb", None),
        P("grp", "pb"),
        P("pb", "grp", None),
        P("pb", None),
        P("pb", "grp"),
        P("pb", "grp", None, None),
        P("pb", "grp", None, None),
    )
    return jax.shard_map(
        shards, mesh=mesh, in_specs=placed, out_specs=P("grp", "pb"), check_vma=False
    )
```
